32 devices in a mesh: row: 8 (over z, x), loop: 4 (over y, core).
Axes of the slice: x: 2, y: 2, z: 4, core: 2. Of those that a mesh axis runs over, the one named last changes fastest.
Arguments:
- pair: bfloat16 [192, 192, 128], P('row', 'loop'), may hold values from -6 to 6
- ln_in_gain: float32 [128], replicated, may hold values from 0.1 to 1.9
- ln_in_bias: float32 [128], replicated, may hold values from -3 to 3
- w_proj: bfloat16 [128, 512], replicated, may hold values from -0.5 to 0.5
- w_gate: bfloat16 [128, 128], replicated, may hold values from -0.5 to 0.5
- ln_out_gain: float32 [128], replicated, may hold values from 0.1 to 1.9
- ln_out_bias: float32 [128], replicated, may hold values from -3 to 3
- w_out: bfloat16 [128, 128], replicated, may hold values from -0.5 to 0.5
Outputs:
- update: bfloat16 [192, 192, 128], P('row', 'loop')
The draws below stay inside these ranges and needn't reach their ends.
All inputs are finite; a program needn't handle non-finite values.
Results may differ from the reference program's by a relative error of at most 0.0055.
Values may be sent and summed in bfloat16 or wider, within the bound.
No kernel may reach another device: no remote copies, remote signals or barrier semaphores. Data moves between devices by JAX's collectives and lax.ppermute only.
A program may use at most 192 MiB of HBM per device.

```python
import jax
import jax.numpy as jnp
from jax import lax

C = 128
H = 128
ROWS_DEV = 24
N = 192


def level_of(rng, dims, split, smallest, largest):
    def one(dim, parts):
        heights = jax.random.uniform(jax.random.fold_in(jax.random.fold_in(rng, 6), dim), (parts,), jnp.float32, smallest / len(split), largest / len(split))
        return jnp.repeat(jnp.exp(heights), dims[dim] // parts).reshape((-1,) + (1,) * (len(dims) - dim - 1))

    level = one(*split[0])
    for cut in split[1:]:
        level = level * one(*cut)
    return level


def gaussian(rng, dims, scale, reach, split=(), dtype=jnp.bfloat16):
    values = jax.random.normal(rng, dims, jnp.float32) * scale
    if len(split) > 0:
        values = level_of(rng, dims, split, -0.22, 0.18) * values
    return jnp.clip(values, min=-reach, max=reach).astype(dtype)


def setup_inputs(seed: int = 0) -> dict:
    key_of = jax.random.split(jax.random.key(seed), 9)
    return {
        "pair": gaussian(key_of[0], (N, N, C), 1.0, 6.0, ((0, 8), (1, 4))),
        "ln_in_gain": jnp.clip(1.0 + 0.18 * jax.random.normal(key_of[1], (C,), jnp.float32), 0.1, 1.9),
        "ln_in_bias": gaussian(key_of[2], (C,), 0.5, 3.0, (), jnp.float32),
        "w_proj": gaussian(key_of[3], (C, 4 * H), C ** -0.5, 0.5),
        "w_gate": gaussian(key_of[4], (C, C), C ** -0.5, 0.5),
        "ln_out_gain": jnp.clip(1.0 + 0.18 * jax.random.normal(key_of[5], (H,), jnp.float32), 0.1, 1.9),
        "ln_out_bias": gaussian(key_of[6], (H,), 0.5, 3.0, (), jnp.float32),
        "w_out": gaussian(key_of[7], (H, C), H ** -0.5, 0.5),
    }


epsilon = 1e-05

def layer_norm(values, gain, bias):
    values = values.astype(jnp.float32)
    center = values - lax.optimization_barrier(jnp.mean(values, axis=-1, keepdims=True))
    spread = lax.optimization_barrier(jnp.mean(center * center, axis=-1, keepdims=True))
    return center * lax.rsqrt(spread + epsilon) * gain + bias

def reference(pair, ln_in_gain, ln_in_bias, w_proj, w_gate, ln_out_gain, ln_out_bias, w_out):
    normed = layer_norm(pair, ln_in_gain, ln_in_bias).astype(jnp.bfloat16)
    projected = jnp.dot(normed.reshape(N * N, C), w_proj, preferred_element_type=jnp.float32)
    projected = projected.reshape(N, N, 4 * H)
    left = (jax.nn.sigmoid(projected[:, :, :H]) * projected[:, :, H:2 * H]).astype(jnp.bfloat16)
    right = (jax.nn.sigmoid(projected[:, :, 2 * H:3 * H]) * projected[:, :, 3 * H:]).astype(jnp.bfloat16)
    right_wide = right.astype(jnp.float32)

    def one_block(first):
        left_part = lax.dynamic_slice_in_dim(left, first, ROWS_DEV, 1).astype(jnp.float32)
        triangle = jnp.einsum('kic,kjc->ijc', left_part, right_wide)
        mixed = layer_norm(triangle, ln_out_gain, ln_out_bias).astype(jnp.bfloat16)
        outgoing = jnp.dot(mixed.reshape(ROWS_DEV * N, H), w_out, preferred_element_type=jnp.float32)
        normed_part = lax.dynamic_slice_in_dim(normed, first, ROWS_DEV, 0).reshape(ROWS_DEV * N, C)
        gating = jax.nn.sigmoid(jnp.dot(normed_part, w_gate, preferred_element_type=jnp.float32))
        return (gating * outgoing).astype(jnp.bfloat16).reshape(ROWS_DEV, N, C)
    starts = (jnp.arange(N // ROWS_DEV) * ROWS_DEV).astype(jnp.int32)
    blocks = lax.map(one_block, starts)
    return blocks.reshape(N, N, C)
```

```python
import jax
import jax.numpy as jnp
from jax import lax
from jax.sharding import PartitionSpec as P

epsilon = 1e-05
axes = ("row", "loop")


def on_device(rows, loops, pair, ln_in_gain, ln_in_bias, w_proj, w_gate, ln_out_gain, ln_out_bias, w_out):
    local_rows, local_cols, channels = pair.shape
    hidden = w_out.shape[0]
    devices = rows * loops
    share = hidden // devices
    places = local_rows * local_cols

    values = pair.reshape(places, channels).astype(jnp.float32)
    center = values - jnp.mean(values, axis=-1, keepdims=True)
    spread = jnp.mean(center * center, axis=-1, keepdims=True)
    normed = (center * lax.rsqrt(spread + epsilon) * ln_in_gain + ln_in_bias).astype(jnp.bfloat16)

    weights = w_proj.reshape(channels, 2, 2, devices, share).transpose(2, 3, 1, 4, 0)
    projected = lax.dot_general(
        weights.reshape(4 * hidden, channels),
        normed,
        (((1,), (1,)), ((), ())),
        preferred_element_type=jnp.float32,
    )
    sides = (jax.nn.sigmoid(projected[: 2 * hidden]) * projected[2 * hidden :]).astype(jnp.bfloat16)
    sides = lax.all_to_all(
        sides.reshape(devices, 2 * share, places), axes, split_axis=0, concat_axis=0
    )
    sides = sides.reshape(rows, loops, 2, share, local_rows, local_cols).transpose(2, 3, 0, 4, 1, 5)
    sides = sides.reshape(2, share, rows * local_rows, loops * local_cols)
    triangle = lax.dot_general(
        sides[0], sides[1], (((1,), (1,)), ((0,), (0,))), preferred_element_type=jnp.float32
    ).astype(jnp.bfloat16)
    triangle = triangle.reshape(share, rows, local_rows, loops, local_cols).transpose(1, 3, 0, 2, 4)
    triangle = lax.all_to_all(
        triangle.reshape(devices, share, places), axes, split_axis=0, concat_axis=0
    )
    triangle = triangle.reshape(hidden, places).astype(jnp.float32)
    center = triangle - jnp.mean(triangle, axis=0, keepdims=True)
    spread = jnp.mean(center * center, axis=0, keepdims=True)
    mixed = center * lax.rsqrt(spread + epsilon) * ln_out_gain[:, None] + ln_out_bias[:, None]
    outgoing = lax.dot_general(
        mixed.astype(jnp.bfloat16),
        w_out,
        (((0,), (0,)), ((), ())),
        preferred_element_type=jnp.float32,
    )
    gating = jax.nn.sigmoid(jnp.dot(normed, w_gate, preferred_element_type=jnp.float32))
    return (gating * outgoing).astype(jnp.bfloat16).reshape(local_rows, local_cols, channels)


def solution(mesh):
    rows, loops = mesh.shape["row"], mesh.shape["loop"]
    return jax.shard_map(
        lambda *arrays: on_device(rows, loops, *arrays),
        mesh=mesh,
        in_specs=(P("row", "loop", None), P(), P(), P(), P(), P(), P(), P()),
        out_specs=P("row", "loop", None),
        check_vma=False,
    )
```

```python
import functools

import jax
import jax.numpy as jnp
from jax import lax
from jax.experimental import pallas as pl
from jax.experimental.pallas import tpu as pltpu
from jax.sharding import PartitionSpec as P

epsilon = 1e-05
axes = ("row", "loop")
in_vmem = pl.BlockSpec(memory_space=pltpu.VMEM)
in_hbm = pl.BlockSpec(memory_space=pltpu.HBM)
vmem_bytes = 48 * 2**20
all_vmem_bytes = 66 * 10**6


def sides_kernel(chunk, devices, pair_any, gain_any, bias_any, w_any, out_ref, pair_ref, gain_ref, bias_ref, w_ref, sems):
    places = pair_ref.shape[0]
    wide = w_ref.shape[1]
    half, hidden = wide // 2, wide // 4
    share = hidden // devices
    starts = list(range(0, places, chunk))
    copies = [
        pltpu.make_async_copy(w_any, w_ref, sems.at[0]),
        pltpu.make_async_copy(gain_any, gain_ref, sems.at[1]),
        pltpu.make_async_copy(bias_any, bias_ref, sems.at[2]),
    ]
    for n, first in enumerate(starts):
        part = pl.ds(first, chunk)
        copies.append(pltpu.make_async_copy(pair_any.at[part], pair_ref.at[part], sems.at[3 + n]))
    for copy in copies:
        copy.start()

    row = lax.broadcasted_iota(jnp.int32, (1, wide), 1)
    value, row = row // half, row % half
    owner, row = row // (2 * share), row % (2 * share)
    column = ((row // share) * 2 + value) * hidden + owner * share + row % share
    source = lax.broadcasted_iota(jnp.int32, (wide, wide), 0)
    pick = jnp.where(source == column, 1.0, 0.0).astype(jnp.bfloat16)
    copies[0].wait()
    weights = jnp.dot(w_ref[...], pick, preferred_element_type=jnp.float32)
    weights = weights.T.astype(jnp.bfloat16)
    copies[1].wait()
    copies[2].wait()
    for n, first in enumerate(starts):
        copies[3 + n].wait()
        values = pair_ref[first : first + chunk, :].astype(jnp.float32)
        center = values - jnp.mean(values, axis=-1, keepdims=True)
        spread = jnp.mean(center * center, axis=-1, keepdims=True)
        normed = center * lax.rsqrt(spread + epsilon) * gain_ref[...] + bias_ref[...]
        projected = lax.dot_general(
            weights,
            normed.astype(jnp.bfloat16),
            (((1,), (1,)), ((), ())),
            preferred_element_type=jnp.float32,
        )
        sides = jax.nn.sigmoid(projected[:half]) * projected[half:]
        out_ref[:, first : first + chunk] = sides.astype(jnp.bfloat16)


def triangle_kernel(rows, loops, local_rows, local_cols, pad, in_ref, out_ref, sides_ref, tri_ref):
    both = in_ref.shape[1]
    share = both // 2
    tokens = rows * local_rows
    tiles = loops * pad // 128
    blank = jnp.zeros((both, pad - local_cols), jnp.float32)

    @pl.loop(0, rows)
    def unpack(r):
        blocks = [in_ref[r * loops + l].astype(jnp.float32) for l in range(loops)]
        for k in range(local_rows):
            line = []
            for block in blocks:
                line.append(block[:, k * local_cols : (k + 1) * local_cols])
                if pad > local_cols:
                    line.append(blank)
            line = jnp.concatenate(line, axis=1)
            for t in range(tiles):
                place = pl.ds(t * both * tokens + r * local_rows + k, both, stride=tokens)
                sides_ref[place, :] = line[:, t * 128 : (t + 1) * 128]

    def matrix(index):
        return jnp.concatenate(
            [sides_ref[pl.ds((t * both + index) * tokens, tokens), :] for t in range(tiles)], axis=1
        ).astype(jnp.bfloat16)

    for c in range(share):
        product = lax.dot_general(
            matrix(c), matrix(share + c), (((0,), (0,)), ((), ())), preferred_element_type=jnp.float32
        )
        for t in range(tiles):
            tri_ref[pl.ds((t * share + c) * loops * pad, loops * pad), :] = product[:, t * 128 : (t + 1) * 128]

    @pl.loop(0, rows)
    def pack(r):
        begin = r * local_rows
        begin = (begin // local_cols) * pad + begin % local_cols
        for l in range(loops):
            first, last = l * pad // 128, -(-(l * pad + local_cols) // 128)
            line = []
            for k in range(local_rows):
                here = [
                    tri_ref[pl.ds(t * share * loops * pad + begin + k, share, stride=loops * pad), :]
                    for t in range(first, last)
                ]
                offset = l * pad - first * 128
                line.append(jnp.concatenate(here, axis=1)[:, offset : offset + local_cols])
            out_ref[r * loops + l] = jnp.concatenate(line, axis=1).astype(jnp.bfloat16)


def line_triangle_kernel(rows, loops, local_rows, local_cols, in_ref, out_ref, sides_ref, tri_ref):
    both = in_ref.shape[1]
    share = both // 2
    places = local_rows * local_cols
    tokens = rows * local_rows
    pairs = loops // 2
    group = local_cols // local_rows
    lane = lax.broadcasted_iota(jnp.int32, (both, 128), 1)

    @pl.loop(0, rows, unroll=4 if rows % 4 == 0 else 1)
    def unpack(r):
        for pair in range(pairs):
            one = in_ref[r * loops + 2 * pair].astype(jnp.float32)
            two = in_ref[r * loops + 2 * pair + 1].astype(jnp.float32)
            one = [one[:, u * 128 : (u + 1) * 128] for u in range(places // 128)]
            two = [pltpu.roll(two[:, u * 128 : (u + 1) * 128], 64, 1) for u in range(places // 128)]
            for k in range(local_rows):
                u, offset = divmod(k * local_cols, 128)
                a, b = one[u], two[u]
                if offset + local_cols > 128:
                    a = jnp.where(lane >= offset, a, one[u + 1])
                    b = jnp.where(lane < 64, b, two[u + 1])
                if offset <= 64:
                    is_a = (lane >= offset) & (lane < offset + 64)
                else:
                    is_a = (lane >= offset) | (lane < offset - 64)
                line = pltpu.roll(jnp.where(is_a, a, b), (128 - offset) % 128, 1)
                sides_ref[pl.ds(pair * both * tokens + r * local_rows + k, both, stride=tokens), :] = line

    def matrix(index):
        return jnp.concatenate(
            [sides_ref[pl.ds((t * both + index) * tokens, tokens), :] for t in range(pairs)], axis=1
        ).astype(jnp.bfloat16)

    for c in range(share):
        product = lax.dot_general(
            matrix(c), matrix(share + c), (((0,), (0,)), ((), ())), preferred_element_type=jnp.float32
        )
        for t in range(pairs):
            for l in range(loops):
                for h in range(group):
                    place = (((t * group + h) * share + c) * loops + l) * local_rows
                    first = l * 64 + h * local_rows
                    tri_ref[place : place + local_rows, :] = product[
                        first : first + local_rows, t * 128 : (t + 1) * 128
                    ]

    turned = (lane[: group * share] + 64) % 128

    @pl.loop(0, loops, unroll=True)
    def pack(l):
        for t in range(pairs):
            lines = []
            for k in range(local_rows):
                place = t * group * share * loops * local_rows + l * local_rows + k
                line = tri_ref[pl.ds(place, group * share, stride=loops * local_rows), :]
                lines.append(pltpu.roll(line, k * local_cols % 128, 1))
            for side in range(2):
                at = turned if side else lane[: group * share]
                whole = []
                for u in range(places // 128):
                    first, last = u * 128 // local_cols, ((u + 1) * 128 - 1) // local_cols
                    tile = lines[first]
                    for k in range(first + 1, last + 1):
                        tile = jnp.where(at >= k * local_cols - u * 128, lines[k], tile)
                    whole.append(pltpu.roll(tile, 64, 1) if side else tile)
                whole = jnp.concatenate(whole, axis=1)
                for h in range(group):
                    out_ref[(l * group + h) * loops + 2 * t + side] = whole[
                        h * share : (h + 1) * share
                    ].astype(jnp.bfloat16)


def chunk_of(places):
    return next((c for c in (512, 384, 256, 128) if places % c == 0), places)


def make_sides(pair, gain, bias, w_proj, devices):
    places, channels = pair.shape
    wide = w_proj.shape[1]
    chunk = chunk_of(places)
    return pl.pallas_call(
        functools.partial(sides_kernel, chunk, devices),
        out_shape=jax.ShapeDtypeStruct((wide // 2, places), jnp.bfloat16),
        in_specs=[in_hbm] * 4,
        out_specs=in_vmem,
        scratch_shapes=[
            pltpu.VMEM(pair.shape, pair.dtype),
            pltpu.VMEM(gain.shape, gain.dtype),
            pltpu.VMEM(bias.shape, bias.dtype),
            pltpu.VMEM(w_proj.shape, w_proj.dtype),
            pltpu.SemaphoreType.DMA((3 + places // chunk,)),
        ],
        compiler_params=pltpu.CompilerParams(vmem_limit_bytes=all_vmem_bytes),
        name="sides",
    )(pair, gain, bias, w_proj)


def gating_kernel(pair_ref, in_gain_ref, in_bias_ref, w_gate_ref, out_gain_ref, out_bias_ref, w_out_ref, _, gating_ref, columns_ref, w_ref):
    values = pair_ref[...].astype(jnp.float32)
    center = values - jnp.mean(values, axis=-1, keepdims=True)
    spread = jnp.mean(center * center, axis=-1, keepdims=True)
    normed = center * lax.rsqrt(spread + epsilon) * in_gain_ref[...] + in_bias_ref[...]
    gate = jnp.dot(normed.astype(jnp.bfloat16), w_gate_ref[...], preferred_element_type=jnp.float32)
    gating_ref[...] = jax.nn.sigmoid(gate)
    hidden = w_out_ref.shape[0]
    columns_ref[0] = jnp.broadcast_to(out_gain_ref[...], (128, hidden)).T
    columns_ref[1] = jnp.broadcast_to(out_bias_ref[...], (128, hidden)).T
    w_ref[...] = w_out_ref[...]


def make_gating(pair, in_gain, in_bias, w_gate, out_gain, out_bias, w_out, after):
    places, channels = pair.shape
    hidden = w_out.shape[0]
    return pl.pallas_call(
        gating_kernel,
        out_shape=(
            jax.ShapeDtypeStruct((places, channels), jnp.float32),
            jax.ShapeDtypeStruct((2, hidden, 128), jnp.float32),
            jax.ShapeDtypeStruct(w_out.shape, w_out.dtype),
        ),
        in_specs=[in_vmem] * 7 + [in_hbm],
        out_specs=[in_vmem] * 3,
        compiler_params=pltpu.CompilerParams(vmem_limit_bytes=vmem_bytes),
        cost_estimate=pl.CostEstimate(
            flops=2 * places * channels * channels, bytes_accessed=6 * places * channels, transcendentals=places * channels
        ),
        name="gating",
    )(pair, in_gain, in_bias, w_gate, out_gain, out_bias, w_out, after)


def update_kernel(chunk, tri_ref, gating_ref, columns_ref, w_ref, out_any, out_ref, sems):
    places = tri_ref.shape[1]
    copies = []
    for n, first in enumerate(range(0, places, chunk)):
        part = pl.ds(first, chunk)
        values = tri_ref[:, first : first + chunk].astype(jnp.float32)
        center = values - jnp.mean(values, axis=0, keepdims=True)
        spread = jnp.mean(center * center, axis=0, keepdims=True)
        mixed = center * lax.rsqrt(spread + epsilon) * columns_ref[0][:, :1] + columns_ref[1][:, :1]
        outgoing = lax.dot_general(
            mixed.astype(jnp.bfloat16), w_ref[...], (((0,), (0,)), ((), ())), preferred_element_type=jnp.float32
        )
        out_ref[part, :] = (gating_ref[part, :] * outgoing).astype(jnp.bfloat16)
        copies.append(pltpu.make_async_copy(out_ref.at[part], out_any.at[part], sems.at[n]))
        copies[-1].start()
    for copy in copies:
        copy.wait()


def make_update(triangle, gating, columns, w_out):
    places, channels = gating.shape
    chunk = chunk_of(places)
    return pl.pallas_call(
        functools.partial(update_kernel, chunk),
        out_shape=jax.ShapeDtypeStruct((places, channels), jnp.bfloat16),
        in_specs=[in_vmem] * 4,
        out_specs=in_hbm,
        scratch_shapes=[
            pltpu.VMEM((places, channels), jnp.bfloat16),
            pltpu.SemaphoreType.DMA((places // chunk,)),
        ],
        compiler_params=pltpu.CompilerParams(vmem_limit_bytes=vmem_bytes),
        name="update",
    )(triangle, gating, columns, w_out)


def make_triangle(sides, rows, loops, local_rows, local_cols):
    devices, both, places = sides.shape
    share = both // 2
    pad = 64 if local_cols <= 64 else -(-local_cols // 128) * 128
    tokens, tiles = rows * local_rows, loops * pad // 128
    kernel = functools.partial(triangle_kernel, rows, loops, local_rows, local_cols, pad)
    tri_rows = tiles * share * loops * pad
    if (
        local_cols <= 64
        and local_cols % local_rows == 0
        and local_rows % 8 == 0
        and places % 128 == 0
        and loops % 2 == 0
        and both * local_cols <= 16 * local_rows
        and both <= 8
    ):
        kernel = functools.partial(line_triangle_kernel, rows, loops, local_rows, local_cols)
        tri_rows = tiles * share * tokens
    return pl.pallas_call(
        kernel,
        out_shape=jax.ShapeDtypeStruct((devices, share, places), jnp.bfloat16),
        in_specs=[in_vmem],
        out_specs=in_vmem,
        scratch_shapes=[
            pltpu.VMEM((tiles * both * tokens, 128), jnp.float32),
            pltpu.VMEM((tri_rows, 128), jnp.float32),
        ],
        compiler_params=pltpu.CompilerParams(vmem_limit_bytes=vmem_bytes),
        name="triangle",
    )(sides)


def on_device(rows, loops, pair, ln_in_gain, ln_in_bias, w_proj, w_gate, ln_out_gain, ln_out_bias, w_out):
    local_rows, local_cols, channels = pair.shape
    hidden = w_out.shape[0]
    devices = rows * loops
    share = hidden // devices
    places = local_rows * local_cols

    pair = pair.reshape(places, channels)
    in_gain, in_bias = ln_in_gain[None], ln_in_bias[None]
    sides = make_sides(pair, in_gain, in_bias, w_proj, devices)
    sides = lax.all_to_all(
        sides.reshape(devices, 2 * share, places), axes, split_axis=0, concat_axis=0
    )
    triangle = make_triangle(sides, rows, loops, local_rows, local_cols)
    gating, columns, w_out = make_gating(
        pair, in_gain, in_bias, w_gate, ln_out_gain[None], ln_out_bias[None], w_out, triangle
    )
    triangle = lax.all_to_all(triangle, axes, split_axis=0, concat_axis=0)
    update = make_update(triangle.reshape(hidden, places), gating, columns, w_out)
    return update.reshape(local_rows, local_cols, channels)


def solution(mesh):
    rows, loops = mesh.shape["row"], mesh.shape["loop"]
    return jax.shard_map(
        lambda *arrays: on_device(rows, loops, *arrays),
        mesh=mesh,
        in_specs=(P("row", "loop", None), P(), P(), P(), P(), P(), P(), P()),
        out_specs=P("row", "loop", None),
        check_vma=False,
    )
```

```python
import functools

import jax
import jax.numpy as jnp
from jax import lax
from jax.experimental import pallas as pl
from jax.experimental.pallas import tpu as pltpu
from jax.sharding import PartitionSpec as P

epsilon = 1e-05
axes = ("row", "loop")
in_vmem = pl.BlockSpec(memory_space=pltpu.VMEM)
in_hbm = pl.BlockSpec(memory_space=pltpu.HBM)
vmem_bytes = 48 * 2**20
all_vmem_bytes = 66 * 10**6


def sides_kernel(chunk, devices, pair_any, gain_any, bias_any, w_any, out_ref, pair_ref, gain_ref, bias_ref, w_ref, sems):
    places = pair_ref.shape[0]
    wide = w_ref.shape[1]
    half, hidden = wide // 2, wide // 4
    share = hidden // devices
    starts = list(range(0, places, chunk))
    copies = [
        pltpu.make_async_copy(w_any, w_ref, sems.at[0]),
        pltpu.make_async_copy(gain_any, gain_ref, sems.at[1]),
        pltpu.make_async_copy(bias_any, bias_ref, sems.at[2]),
    ]
    for n, first in enumerate(starts):
        part = pl.ds(first, chunk)
        copies.append(pltpu.make_async_copy(pair_any.at[part], pair_ref.at[part], sems.at[3 + n]))
    for copy in copies:
        copy.start()

    row = lax.broadcasted_iota(jnp.int32, (1, wide), 1)
    value, row = row // half, row % half
    owner, row = row // (2 * share), row % (2 * share)
    column = ((row // share) * 2 + value) * hidden + owner * share + row % share
    source = lax.broadcasted_iota(jnp.int32, (wide, wide), 0)
    pick = jnp.where(source == column, 1.0, 0.0).astype(jnp.bfloat16)
    copies[0].wait()
    weights = jnp.dot(w_ref[...], pick, preferred_element_type=jnp.float32)
    weights = weights.T.astype(jnp.bfloat16)
    copies[1].wait()
    copies[2].wait()
    for n, first in enumerate(starts):
        copies[3 + n].wait()
        values = pair_ref[first : first + chunk, :].astype(jnp.float32)
        center = values - jnp.mean(values, axis=-1, keepdims=True)
        spread = jnp.mean(center * center, axis=-1, keepdims=True)
        normed = center * lax.rsqrt(spread + epsilon) * gain_ref[...] + bias_ref[...]
        projected = lax.dot_general(
            weights,
            normed.astype(jnp.bfloat16),
            (((1,), (1,)), ((), ())),
            preferred_element_type=jnp.float32,
        )
        sides = jax.nn.sigmoid(projected[:half]) * projected[half:]
        out_ref[:, first : first + chunk] = sides.astype(jnp.bfloat16)


def triangle_kernel(rows, loops, local_rows, local_cols, pad, in_ref, out_ref, sides_ref, tri_ref):
    both = in_ref.shape[1]
    share = both // 2
    tokens = rows * local_rows
    tiles = loops * pad // 128
    blank = jnp.zeros((both, pad - local_cols), jnp.float32)

    @pl.loop(0, rows)
    def unpack(r):
        blocks = [in_ref[r * loops + l].astype(jnp.float32) for l in range(loops)]
        for k in range(local_rows):
            line = []
            for block in blocks:
                line.append(block[:, k * local_cols : (k + 1) * local_cols])
                if pad > local_cols:
                    line.append(blank)
            line = jnp.concatenate(line, axis=1)
            for t in range(tiles):
                place = pl.ds(t * both * tokens + r * local_rows + k, both, stride=tokens)
                sides_ref[place, :] = line[:, t * 128 : (t + 1) * 128]

    def matrix(index):
        return jnp.concatenate(
            [sides_ref[pl.ds((t * both + index) * tokens, tokens), :] for t in range(tiles)], axis=1
        ).astype(jnp.bfloat16)

    for c in range(share):
        product = lax.dot_general(
            matrix(c), matrix(share + c), (((0,), (0,)), ((), ())), preferred_element_type=jnp.float32
        )
        for t in range(tiles):
            tri_ref[pl.ds((t * share + c) * loops * pad, loops * pad), :] = product[:, t * 128 : (t + 1) * 128]

    @pl.loop(0, rows)
    def pack(r):
        begin = r * local_rows
        begin = (begin // local_cols) * pad + begin % local_cols
        for l in range(loops):
            first, last = l * pad // 128, -(-(l * pad + local_cols) // 128)
            line = []
            for k in range(local_rows):
                here = [
                    tri_ref[pl.ds(t * share * loops * pad + begin + k, share, stride=loops * pad), :]
                    for t in range(first, last)
                ]
                offset = l * pad - first * 128
                line.append(jnp.concatenate(here, axis=1)[:, offset : offset + local_cols])
            out_ref[r * loops + l] = jnp.concatenate(line, axis=1).astype(jnp.bfloat16)


def line_offsets(local_rows, local_cols):
    return sorted({k * local_cols % 128 for k in range(local_rows)})


def line_triangle_kernel(rows, loops, local_rows, local_cols, in_ref, shifts_ref, out_ref, sides_ref, tri_ref):
    both = in_ref.shape[1]
    share = both // 2
    places = local_rows * local_cols
    tokens = rows * local_rows
    pairs = loops // 2
    group = local_cols // local_rows
    height = tokens + 8
    block = loops * local_rows + 8
    lane = lax.broadcasted_iota(jnp.int32, (rows * both, 128), 1)

    blocks = [jnp.concatenate([in_ref[r * loops + l] for r in range(rows)], axis=0) for l in range(loops)]
    for n, offset in enumerate(line_offsets(local_rows, local_cols)):
        stack, target = [], []
        for pair in range(pairs):
            for k in range(local_rows):
                u = k * local_cols // 128
                if k * local_cols % 128 != offset:
                    continue
                line = []
                for side in blocks[2 * pair : 2 * pair + 2]:
                    tile = side[:, u * 128 : (u + 1) * 128]
                    if offset + local_cols > 128:
                        tile = jnp.where(lane >= offset, tile, side[:, (u + 1) * 128 : (u + 2) * 128])
                    line.append(tile)
                stack.append(jnp.concatenate(line, axis=1))
                target.append(pair * both * height + k)
        lines = jnp.dot(jnp.concatenate(stack, axis=0), shifts_ref[n], preferred_element_type=jnp.float32)
        for m, place in enumerate(target):
            for r in range(rows):
                first = (m * rows + r) * both
                sides_ref[pl.ds(place + r * local_rows, both, stride=height), :] = lines[first : first + both]

    def matrix(index):
        return jnp.concatenate(
            [sides_ref[pl.ds((t * both + index) * height, tokens), :] for t in range(pairs)], axis=1
        ).astype(jnp.bfloat16)

    for c in range(share):
        product = lax.dot_general(
            matrix(c), matrix(share + c), (((0,), (0,)), ((), ())), preferred_element_type=jnp.float32
        )
        for t in range(pairs):
            for h in range(group):
                for l in range(loops):
                    place = ((t * group + h) * share + c) * block + l * local_rows
                    first = l * 64 + h * local_rows
                    tri_ref[place : place + local_rows, :] = product[
                        first : first + local_rows, t * 128 : (t + 1) * 128
                    ]

    lane = lax.broadcasted_iota(jnp.int32, (group * share, 128), 1)
    turned = (lane + 64) % 128

    @pl.loop(0, loops, unroll=True)
    def pack(l):
        for t in range(pairs):
            lines = []
            for k in range(local_rows):
                place = t * group * share * block + l * local_rows + k
                line = tri_ref[pl.ds(place, group * share, stride=block), :]
                lines.append(pltpu.roll(line, k * local_cols % 128, 1))
            for side in range(2):
                at = turned if side else lane
                whole = []
                for u in range(places // 128):
                    first, last = u * 128 // local_cols, ((u + 1) * 128 - 1) // local_cols
                    tile = lines[first]
                    for k in range(first + 1, last + 1):
                        tile = jnp.where(at >= k * local_cols - u * 128, lines[k], tile)
                    whole.append(pltpu.roll(tile, 64, 1) if side else tile)
                whole = jnp.concatenate(whole, axis=1)
                for h in range(group):
                    out_ref[(l * group + h) * loops + 2 * t + side] = whole[
                        h * share : (h + 1) * share
                    ].astype(jnp.bfloat16)


def chunk_of(places):
    return next((c for c in (512, 384, 256, 128) if places % c == 0), places)


def make_sides(pair, gain, bias, w_proj, devices):
    places, channels = pair.shape
    wide = w_proj.shape[1]
    chunk = chunk_of(places)
    return pl.pallas_call(
        functools.partial(sides_kernel, chunk, devices),
        out_shape=jax.ShapeDtypeStruct((wide // 2, places), jnp.bfloat16),
        in_specs=[in_hbm] * 4,
        out_specs=in_vmem,
        scratch_shapes=[
            pltpu.VMEM(pair.shape, pair.dtype),
            pltpu.VMEM(gain.shape, gain.dtype),
            pltpu.VMEM(bias.shape, bias.dtype),
            pltpu.VMEM(w_proj.shape, w_proj.dtype),
            pltpu.SemaphoreType.DMA((3 + places // chunk,)),
        ],
        compiler_params=pltpu.CompilerParams(vmem_limit_bytes=all_vmem_bytes),
        name="sides",
    )(pair, gain, bias, w_proj)


def prepare_kernel(offsets, local_cols, pair_ref, in_gain_ref, in_bias_ref, w_gate_ref, out_gain_ref, out_bias_ref, w_out_ref, _, gating_ref, columns_ref, w_ref, shifts_ref):
    values = pair_ref[...].astype(jnp.float32)
    center = values - jnp.mean(values, axis=-1, keepdims=True)
    spread = jnp.mean(center * center, axis=-1, keepdims=True)
    normed = center * lax.rsqrt(spread + epsilon) * in_gain_ref[...] + in_bias_ref[...]
    gate = jnp.dot(normed.astype(jnp.bfloat16), w_gate_ref[...], preferred_element_type=jnp.float32)
    gating_ref[...] = jax.nn.sigmoid(gate)
    hidden = w_out_ref.shape[0]
    columns_ref[0] = jnp.broadcast_to(out_gain_ref[...], (128, hidden)).T
    columns_ref[1] = jnp.broadcast_to(out_bias_ref[...], (128, hidden)).T
    w_ref[...] = w_out_ref[...]
    source = lax.broadcasted_iota(jnp.int32, (256, 128), 0)
    lane = lax.broadcasted_iota(jnp.int32, (256, 128), 1)
    for n, offset in enumerate(offsets):
        wanted = ((lane & 63) + offset) & 127
        wanted = jnp.where(lane >= 64, wanted + 128, wanted)
        picked = (source == wanted) & ((lane & 63) < local_cols)
        shifts_ref[n] = jnp.where(picked, 1.0, 0.0).astype(jnp.bfloat16)


def make_prepared(pair, in_gain, in_bias, w_gate, out_gain, out_bias, w_out, after, local_rows, local_cols):
    places, channels = pair.shape
    hidden = w_out.shape[0]
    offsets = line_offsets(local_rows, local_cols)
    return pl.pallas_call(
        functools.partial(prepare_kernel, offsets, local_cols),
        out_shape=(
            jax.ShapeDtypeStruct((places, channels), jnp.float32),
            jax.ShapeDtypeStruct((2, hidden, 128), jnp.float32),
            jax.ShapeDtypeStruct(w_out.shape, w_out.dtype),
            jax.ShapeDtypeStruct((len(offsets), 256, 128), jnp.bfloat16),
        ),
        in_specs=[in_vmem] * 7 + [in_hbm],
        out_specs=[in_vmem] * 4,
        compiler_params=pltpu.CompilerParams(vmem_limit_bytes=vmem_bytes),
        cost_estimate=pl.CostEstimate(
            flops=2 * places * channels * channels, bytes_accessed=6 * places * channels, transcendentals=places * channels
        ),
        name="prepare",
    )(pair, in_gain, in_bias, w_gate, out_gain, out_bias, w_out, after)


def update_kernel(chunk, tri_ref, gating_ref, columns_ref, w_ref, out_any, out_ref, sems):
    places = tri_ref.shape[1]
    copies = []
    for n, first in enumerate(range(0, places, chunk)):
        part = pl.ds(first, chunk)
        values = tri_ref[:, first : first + chunk].astype(jnp.float32)
        center = values - jnp.mean(values, axis=0, keepdims=True)
        spread = jnp.mean(center * center, axis=0, keepdims=True)
        mixed = center * lax.rsqrt(spread + epsilon) * columns_ref[0][:, :1] + columns_ref[1][:, :1]
        outgoing = lax.dot_general(
            mixed.astype(jnp.bfloat16), w_ref[...], (((0,), (0,)), ((), ())), preferred_element_type=jnp.float32
        )
        out_ref[part, :] = (gating_ref[part, :] * outgoing).astype(jnp.bfloat16)
        copies.append(pltpu.make_async_copy(out_ref.at[part], out_any.at[part], sems.at[n]))
        copies[-1].start()
    for copy in copies:
        copy.wait()


def make_update(triangle, gating, columns, w_out):
    places, channels = gating.shape
    chunk = chunk_of(places)
    return pl.pallas_call(
        functools.partial(update_kernel, chunk),
        out_shape=jax.ShapeDtypeStruct((places, channels), jnp.bfloat16),
        in_specs=[in_vmem] * 4,
        out_specs=in_hbm,
        scratch_shapes=[
            pltpu.VMEM((places, channels), jnp.bfloat16),
            pltpu.SemaphoreType.DMA((places // chunk,)),
        ],
        compiler_params=pltpu.CompilerParams(vmem_limit_bytes=vmem_bytes),
        name="update",
    )(triangle, gating, columns, w_out)


def make_triangle(sides, shifts, rows, loops, local_rows, local_cols):
    devices, both, places = sides.shape
    share = both // 2
    pad = 64 if local_cols <= 64 else -(-local_cols // 128) * 128
    tokens, tiles = rows * local_rows, loops * pad // 128
    operands = [sides]
    kernel = functools.partial(triangle_kernel, rows, loops, local_rows, local_cols, pad)
    sides_rows = tiles * both * tokens
    tri_rows = tiles * share * loops * pad
    if (
        local_cols <= 64
        and local_cols % local_rows == 0
        and local_rows % 8 == 0
        and places % 128 == 0
        and loops % 2 == 0
        and both * local_cols <= 16 * local_rows
        and both == 8
    ):
        operands.append(shifts)
        kernel = functools.partial(line_triangle_kernel, rows, loops, local_rows, local_cols)
        sides_rows = tiles * both * (tokens + 8)
        tri_rows = tiles * share * (local_cols // local_rows) * (loops * local_rows + 8)
    return pl.pallas_call(
        kernel,
        out_shape=jax.ShapeDtypeStruct((devices, share, places), jnp.bfloat16),
        in_specs=[in_vmem] * len(operands),
        out_specs=in_vmem,
        scratch_shapes=[
            pltpu.VMEM((sides_rows, 128), jnp.float32),
            pltpu.VMEM((tri_rows, 128), jnp.float32),
        ],
        compiler_params=pltpu.CompilerParams(vmem_limit_bytes=vmem_bytes),
        name="triangle",
    )(*operands)


def on_device(rows, loops, pair, ln_in_gain, ln_in_bias, w_proj, w_gate, ln_out_gain, ln_out_bias, w_out):
    local_rows, local_cols, channels = pair.shape
    hidden = w_out.shape[0]
    devices = rows * loops
    share = hidden // devices
    places = local_rows * local_cols

    pair = pair.reshape(places, channels)
    in_gain, in_bias = ln_in_gain[None], ln_in_bias[None]
    sides = make_sides(pair, in_gain, in_bias, w_proj, devices)
    sides = sides.reshape(devices, 2 * share, places)
    gating, columns, w_out, shifts = make_prepared(
        pair, in_gain, in_bias, w_gate, ln_out_gain[None], ln_out_bias[None], w_out, sides, local_rows, local_cols
    )
    sides = lax.all_to_all(sides, axes, split_axis=0, concat_axis=0)
    triangle = make_triangle(sides, shifts, rows, loops, local_rows, local_cols)
    triangle = lax.all_to_all(triangle, axes, split_axis=0, concat_axis=0)
    update = make_update(triangle.reshape(hidden, places), gating, columns, w_out)
    return update.reshape(local_rows, local_cols, channels)


def solution(mesh):
    rows, loops = mesh.shape["row"], mesh.shape["loop"]
    return jax.shard_map(
        lambda *arrays: on_device(rows, loops, *arrays),
        mesh=mesh,
        in_specs=(P("row", "loop", None), P(), P(), P(), P(), P(), P(), P()),
        out_specs=P("row", "loop", None),
        check_vma=False,
    )
```

```python
import functools

import jax
import jax.numpy as jnp
from jax import lax
from jax.experimental import pallas as pl
from jax.experimental.pallas import tpu as pltpu
from jax.sharding import PartitionSpec as P

epsilon = 1e-05
axes = ("row", "loop")
in_vmem = pl.BlockSpec(memory_space=pltpu.VMEM)
in_hbm = pl.BlockSpec(memory_space=pltpu.HBM)
vmem_bytes = 48 * 2**20


def line_offsets(local_rows, local_cols):
    return sorted({k * local_cols % 128 for k in range(local_rows)})


def sides_kernel(devices, offsets, local_cols, *refs):
    given, results, held, sems = refs[:8], refs[8:13], refs[13:21], refs[21]
    out_ref, gating_ref, columns_ref, w_out_t_ref, shifts_ref = results
    copies = [pltpu.make_async_copy(*ends, sems.at[n]) for n, ends in enumerate(zip(given, held))]
    for copy in copies:
        copy.start()
    pair_ref, w_proj_ref, w_gate_ref, in_gain_ref, in_bias_ref, out_gain_ref, out_bias_ref, w_out_ref = held
    wide = w_proj_ref.shape[1]
    half, hidden = wide // 2, wide // 4
    share = hidden // devices

    row = lax.broadcasted_iota(jnp.int32, (1, wide), 1)
    value, row = row // half, row % half
    owner, row = row // (2 * share), row % (2 * share)
    column = ((row // share) * 2 + value) * hidden + owner * share + row % share
    source = lax.broadcasted_iota(jnp.int32, (wide, wide), 0)
    pick = jnp.where(source == column, 1.0, 0.0).astype(jnp.bfloat16)

    source = lax.broadcasted_iota(jnp.int32, (256, 128), 0)
    lane = lax.broadcasted_iota(jnp.int32, (256, 128), 1)
    for n, offset in enumerate(offsets):
        wanted = ((lane & 63) + offset) & 127
        wanted = jnp.where(lane >= 64, wanted + 128, wanted)
        picked = (source == wanted) & ((lane & 63) < local_cols)
        shifts_ref[n] = jnp.where(picked, 1.0, 0.0).astype(jnp.bfloat16)

    for copy in copies:
        copy.wait()
    weights = jnp.dot(w_proj_ref[...], pick, preferred_element_type=jnp.float32).T.astype(jnp.bfloat16)
    weights = jnp.concatenate([weights, w_gate_ref[...].astype(jnp.float32).T.astype(jnp.bfloat16)], axis=0)
    values = pair_ref[...].astype(jnp.float32)
    center = values - jnp.mean(values, axis=-1, keepdims=True)
    spread = jnp.mean(center * center, axis=-1, keepdims=True)
    normed = center * lax.rsqrt(spread + epsilon) * in_gain_ref[...] + in_bias_ref[...]
    projected = lax.dot_general(
        weights, normed.astype(jnp.bfloat16), (((1,), (1,)), ((), ())), preferred_element_type=jnp.float32
    )
    sides = jax.nn.sigmoid(projected[:half]) * projected[half:wide]
    out_ref[...] = sides.astype(jnp.bfloat16)
    gating_ref[...] = jax.nn.sigmoid(projected[wide:])
    columns_ref[0] = jnp.broadcast_to(out_gain_ref[...], (128, hidden)).T
    columns_ref[1] = jnp.broadcast_to(out_bias_ref[...], (128, hidden)).T
    w_out_t_ref[...] = w_out_ref[...].astype(jnp.float32).T.astype(jnp.bfloat16)


def triangle_kernel(rows, loops, local_rows, local_cols, pad, in_ref, out_ref, sides_ref, tri_ref):
    both = in_ref.shape[1]
    share = both // 2
    tokens = rows * local_rows
    tiles = loops * pad // 128
    blank = jnp.zeros((both, pad - local_cols), jnp.float32)

    @pl.loop(0, rows)
    def unpack(r):
        blocks = [in_ref[r * loops + l].astype(jnp.float32) for l in range(loops)]
        for k in range(local_rows):
            line = []
            for block in blocks:
                line.append(block[:, k * local_cols : (k + 1) * local_cols])
                if pad > local_cols:
                    line.append(blank)
            line = jnp.concatenate(line, axis=1)
            for t in range(tiles):
                place = pl.ds(t * both * tokens + r * local_rows + k, both, stride=tokens)
                sides_ref[place, :] = line[:, t * 128 : (t + 1) * 128]

    def matrix(index):
        return jnp.concatenate(
            [sides_ref[pl.ds((t * both + index) * tokens, tokens), :] for t in range(tiles)], axis=1
        ).astype(jnp.bfloat16)

    for c in range(share):
        product = lax.dot_general(
            matrix(c), matrix(share + c), (((0,), (0,)), ((), ())), preferred_element_type=jnp.float32
        )
        for t in range(tiles):
            tri_ref[pl.ds((t * share + c) * loops * pad, loops * pad), :] = product[:, t * 128 : (t + 1) * 128]

    @pl.loop(0, rows)
    def pack(r):
        begin = r * local_rows
        begin = (begin // local_cols) * pad + begin % local_cols
        for l in range(loops):
            first, last = l * pad // 128, -(-(l * pad + local_cols) // 128)
            line = []
            for k in range(local_rows):
                here = [
                    tri_ref[pl.ds(t * share * loops * pad + begin + k, share, stride=loops * pad), :]
                    for t in range(first, last)
                ]
                offset = l * pad - first * 128
                line.append(jnp.concatenate(here, axis=1)[:, offset : offset + local_cols])
            out_ref[r * loops + l] = jnp.concatenate(line, axis=1).astype(jnp.bfloat16)


def line_triangle_kernel(rows, loops, local_rows, local_cols, in_ref, shifts_ref, out_ref, sides_ref, tri_ref):
    both = in_ref.shape[1]
    share = both // 2
    places = local_rows * local_cols
    tokens = rows * local_rows
    pairs = loops // 2
    group = local_cols // local_rows
    height = tokens + 8
    block = loops * local_rows + 8
    lane = lax.broadcasted_iota(jnp.int32, (rows * both, 128), 1)

    blocks = [jnp.concatenate([in_ref[r * loops + l] for r in range(rows)], axis=0) for l in range(loops)]
    for n, offset in enumerate(line_offsets(local_rows, local_cols)):
        stack, target = [], []
        for pair in range(pairs):
            for k in range(local_rows):
                u = k * local_cols // 128
                if k * local_cols % 128 != offset:
                    continue
                line = []
                for side in blocks[2 * pair : 2 * pair + 2]:
                    tile = side[:, u * 128 : (u + 1) * 128]
                    if offset + local_cols > 128:
                        tile = jnp.where(lane >= offset, tile, side[:, (u + 1) * 128 : (u + 2) * 128])
                    line.append(tile)
                stack.append(jnp.concatenate(line, axis=1))
                target.append(pair * both * height + k)
        lines = jnp.dot(jnp.concatenate(stack, axis=0), shifts_ref[n], preferred_element_type=jnp.float32)
        for m, place in enumerate(target):
            for r in range(rows):
                first = (m * rows + r) * both
                sides_ref[pl.ds(place + r * local_rows, both, stride=height), :] = lines[first : first + both]

    def matrix(index):
        return jnp.concatenate(
            [sides_ref[pl.ds((t * both + index) * height, tokens), :] for t in range(pairs)], axis=1
        ).astype(jnp.bfloat16)

    for c in range(share):
        product = lax.dot_general(
            matrix(c), matrix(share + c), (((0,), (0,)), ((), ())), preferred_element_type=jnp.float32
        )
        for t in range(pairs):
            for h in range(group):
                for l in range(loops):
                    place = ((t * group + h) * share + c) * block + l * local_rows
                    first = l * 64 + h * local_rows
                    tri_ref[place : place + local_rows, :] = product[
                        first : first + local_rows, t * 128 : (t + 1) * 128
                    ]

    lane = lax.broadcasted_iota(jnp.int32, (group * share, 128), 1)
    turned = (lane + 64) % 128

    @pl.loop(0, loops, unroll=True)
    def pack(l):
        for t in range(pairs):
            lines = []
            for k in range(local_rows):
                place = t * group * share * block + l * local_rows + k
                line = tri_ref[pl.ds(place, group * share, stride=block), :]
                lines.append(pltpu.roll(line, k * local_cols % 128, 1))
            for side in range(2):
                at = turned if side else lane
                whole = []
                for u in range(places // 128):
                    first, last = u * 128 // local_cols, ((u + 1) * 128 - 1) // local_cols
                    tile = lines[first]
                    for k in range(first + 1, last + 1):
                        tile = jnp.where(at >= k * local_cols - u * 128, lines[k], tile)
                    whole.append(pltpu.roll(tile, 64, 1) if side else tile)
                whole = jnp.concatenate(whole, axis=1)
                for h in range(group):
                    out_ref[(l * group + h) * loops + 2 * t + side] = whole[
                        h * share : (h + 1) * share
                    ].astype(jnp.bfloat16)


def make_sides(devices, local_rows, local_cols, *given):
    places, channels = given[0].shape
    wide = given[1].shape[1]
    hidden = wide // 4
    offsets = line_offsets(local_rows, local_cols)
    return pl.pallas_call(
        functools.partial(sides_kernel, devices, offsets, local_cols),
        out_shape=(
            jax.ShapeDtypeStruct((wide // 2, places), jnp.bfloat16),
            jax.ShapeDtypeStruct((channels, places), jnp.float32),
            jax.ShapeDtypeStruct((2, hidden, 128), jnp.float32),
            jax.ShapeDtypeStruct((channels, hidden), jnp.bfloat16),
            jax.ShapeDtypeStruct((len(offsets), 256, 128), jnp.bfloat16),
        ),
        in_specs=[in_hbm] * len(given),
        out_specs=[in_vmem] * 5,
        scratch_shapes=[pltpu.VMEM(x.shape, x.dtype) for x in given] + [pltpu.SemaphoreType.DMA((len(given),))],
        compiler_params=pltpu.CompilerParams(vmem_limit_bytes=vmem_bytes),
        name="sides",
    )(*[pltpu.with_memory_space_constraint(x, pltpu.HBM) for x in given])


def update_kernel(tri_ref, gating_ref, columns_ref, w_ref, out_ref):
    values = tri_ref[...].astype(jnp.float32)
    center = values - jnp.mean(values, axis=0, keepdims=True)
    spread = jnp.mean(center * center, axis=0, keepdims=True)
    mixed = center * lax.rsqrt(spread + epsilon) * columns_ref[0][:, :1] + columns_ref[1][:, :1]
    outgoing = jnp.dot(w_ref[...], mixed.astype(jnp.bfloat16), preferred_element_type=jnp.float32)
    out_ref[...] = (gating_ref[...] * outgoing).T.astype(jnp.bfloat16)


def make_update(triangle, gating, columns, w_out_t):
    channels, places = gating.shape
    return pl.pallas_call(
        update_kernel,
        out_shape=jax.ShapeDtypeStruct((places, channels), jnp.bfloat16),
        in_specs=[in_vmem] * 4,
        out_specs=in_vmem,
        compiler_params=pltpu.CompilerParams(vmem_limit_bytes=vmem_bytes),
        name="update",
    )(triangle, gating, columns, w_out_t)


def make_triangle(sides, shifts, rows, loops, local_rows, local_cols):
    devices, both, places = sides.shape
    share = both // 2
    pad = 64 if local_cols <= 64 else -(-local_cols // 128) * 128
    tokens, tiles = rows * local_rows, loops * pad // 128
    operands = [sides]
    kernel = functools.partial(triangle_kernel, rows, loops, local_rows, local_cols, pad)
    sides_rows = tiles * both * tokens
    tri_rows = tiles * share * loops * pad
    if (
        local_cols <= 64
        and local_cols % local_rows == 0
        and local_rows % 8 == 0
        and places % 128 == 0
        and loops % 2 == 0
        and both * local_cols <= 16 * local_rows
        and both == 8
    ):
        operands.append(shifts)
        kernel = functools.partial(line_triangle_kernel, rows, loops, local_rows, local_cols)
        sides_rows = tiles * both * (tokens + 8)
        tri_rows = tiles * share * (local_cols // local_rows) * (loops * local_rows + 8)
    return pl.pallas_call(
        kernel,
        out_shape=jax.ShapeDtypeStruct((devices, share, places), jnp.bfloat16),
        in_specs=[in_vmem] * len(operands),
        out_specs=in_vmem,
        scratch_shapes=[
            pltpu.VMEM((sides_rows, 128), jnp.float32),
            pltpu.VMEM((tri_rows, 128), jnp.float32),
        ],
        compiler_params=pltpu.CompilerParams(vmem_limit_bytes=vmem_bytes),
        name="triangle",
    )(*operands)


def on_device(rows, loops, pair, ln_in_gain, ln_in_bias, w_proj, w_gate, ln_out_gain, ln_out_bias, w_out):
    local_rows, local_cols, channels = pair.shape
    hidden = w_out.shape[0]
    devices = rows * loops
    share = hidden // devices
    places = local_rows * local_cols

    pair = pair.reshape(places, channels)
    sides, gating, columns, w_out_t, shifts = make_sides(
        devices,
        local_rows,
        local_cols,
        pair,
        w_proj,
        w_gate,
        ln_in_gain[None],
        ln_in_bias[None],
        ln_out_gain[None],
        ln_out_bias[None],
        w_out,
    )
    sides = lax.all_to_all(
        sides.reshape(devices, 2 * share, places), axes, split_axis=0, concat_axis=0
    )
    triangle = make_triangle(sides, shifts, rows, loops, local_rows, local_cols)
    triangle = lax.all_to_all(triangle, axes, split_axis=0, concat_axis=0)
    update = make_update(triangle.reshape(hidden, places), gating, columns, w_out_t)
    return update.reshape(local_rows, local_cols, channels)


def solution(mesh):
    rows, loops = mesh.shape["row"], mesh.shape["loop"]
    return jax.shard_map(
        lambda *arrays: on_device(rows, loops, *arrays),
        mesh=mesh,
        in_specs=(P("row", "loop", None), P(), P(), P(), P(), P(), P(), P()),
        out_specs=P("row", "loop", None),
        check_vma=False,
    )
```

```python
import functools
import math

import jax
import jax.numpy as jnp
from jax import lax
from jax.experimental import pallas as pl
from jax.experimental.pallas import tpu as pltpu
from jax.sharding import Mesh
from jax.sharding import PartitionSpec as P

epsilon = 1e-05
in_vmem = pl.BlockSpec(memory_space=pltpu.VMEM)
in_hbm = pl.BlockSpec(memory_space=pltpu.HBM)
vmem_bytes = 48 * 2**20


def line_offsets(local_rows, local_cols):
    return sorted({k * local_cols % 128 for k in range(local_rows)})


def line_tiles(local_cols):
    tiles = math.lcm(local_cols, 128) // 128
    return [(u * 128 // local_cols, ((u + 1) * 128 - 1) // local_cols) for u in range(tiles)]


def in_lines(rows, loops, share, local_rows, local_cols):
    return (
        local_cols <= 64
        and local_cols % local_rows == 0
        and local_rows % 8 == 0
        and local_rows % (math.lcm(local_cols, 128) // local_cols) == 0
        and loops % 2 == 0
        and rows * local_rows == loops * local_cols
        and share % 8 == 0
    )


def sides_kernel(owners, local_rows, local_cols, *refs):
    given, results, held, sems = refs[:8], refs[8:14], refs[14:22], refs[22]
    out_ref, gating_ref, columns_ref, w_out_t_ref, shifts_ref, returns_ref = results
    copies = [pltpu.make_async_copy(*ends, sems.at[n]) for n, ends in enumerate(zip(given, held))]
    for copy in copies:
        copy.start()
    pair_ref, w_proj_ref, w_gate_ref, in_gain_ref, in_bias_ref, out_gain_ref, out_bias_ref, w_out_ref = held
    wide = w_proj_ref.shape[1]
    half, hidden = wide // 2, wide // 4
    share = hidden // owners

    row = lax.broadcasted_iota(jnp.int32, (1, wide), 1)
    value, row = row // half, row % half
    owner, row = row // (2 * share), row % (2 * share)
    column = ((row // share) * 2 + value) * hidden + owner * share + row % share
    source = lax.broadcasted_iota(jnp.int32, (wide, wide), 0)
    pick = jnp.where(source == column, 1.0, 0.0).astype(jnp.bfloat16)

    source = lax.broadcasted_iota(jnp.int32, (256, 128), 0)
    lane = lax.broadcasted_iota(jnp.int32, (256, 128), 1)
    for n, offset in enumerate(line_offsets(local_rows, local_cols)):
        wanted = ((lane & 63) + offset) & 127
        wanted = jnp.where(lane >= 64, wanted + 128, wanted)
        picked = (source == wanted) & ((lane & 63) < local_cols)
        shifts_ref[n] = jnp.where(picked, 1.0, 0.0).astype(jnp.bfloat16)

    source = lax.broadcasted_iota(jnp.int32, (128, 256), 0)
    lane = lax.broadcasted_iota(jnp.int32, (128, 256), 1)
    begin = 0
    for u, (first, last) in enumerate(line_tiles(local_cols)):
        for k in range(first, last + 1):
            inside = (lane & 127) + (u * 128 - k * local_cols)
            wanted = jnp.where(lane >= 128, inside + 64, inside)
            picked = (source == wanted) & (inside >= 0) & (inside < local_cols)
            returns_ref[begin : begin + 128, :] = jnp.where(picked, 1.0, 0.0).astype(jnp.bfloat16)
            begin += 128

    for copy in copies:
        copy.wait()
    weights = jnp.dot(w_proj_ref[...], pick, preferred_element_type=jnp.float32).T.astype(jnp.bfloat16)
    weights = jnp.concatenate([weights, w_gate_ref[...].astype(jnp.float32).T.astype(jnp.bfloat16)], axis=0)
    values = pair_ref[...].astype(jnp.float32)
    center = values - jnp.mean(values, axis=-1, keepdims=True)
    spread = jnp.mean(center * center, axis=-1, keepdims=True)
    normed = center * lax.rsqrt(spread + epsilon) * in_gain_ref[...] + in_bias_ref[...]
    projected = lax.dot_general(
        weights, normed.astype(jnp.bfloat16), (((1,), (1,)), ((), ())), preferred_element_type=jnp.float32
    )
    sides = jax.nn.sigmoid(projected[:half]) * projected[half:wide]
    out_ref[...] = sides.astype(jnp.bfloat16)
    gating_ref[...] = jax.nn.sigmoid(projected[wide:])
    columns_ref[0] = jnp.broadcast_to(out_gain_ref[...], (128, hidden)).T
    columns_ref[1] = jnp.broadcast_to(out_bias_ref[...], (128, hidden)).T
    w_out_t_ref[...] = w_out_ref[...].astype(jnp.float32).T.astype(jnp.bfloat16)


def triangle_kernel(rows, inner, loops, local_rows, local_cols, pad, in_ref, out_ref, sides_ref, tri_ref):
    both = in_ref.shape[1]
    share = both // 2
    depth = inner * local_rows
    tiles = loops * pad // 128
    blank = jnp.zeros((both, pad - local_cols), jnp.float32)

    @pl.loop(0, inner)
    def unpack(r):
        blocks = [in_ref[r * loops + l].astype(jnp.float32) for l in range(loops)]
        for k in range(local_rows):
            line = []
            for block in blocks:
                line.append(block[:, k * local_cols : (k + 1) * local_cols])
                if pad > local_cols:
                    line.append(blank)
            line = jnp.concatenate(line, axis=1)
            for t in range(tiles):
                place = pl.ds(t * both * depth + r * local_rows + k, both, stride=depth)
                sides_ref[place, :] = line[:, t * 128 : (t + 1) * 128]

    def matrix(index):
        return jnp.concatenate(
            [sides_ref[pl.ds((t * both + index) * depth, depth), :] for t in range(tiles)], axis=1
        ).astype(jnp.bfloat16)

    for c in range(share):
        product = lax.dot_general(
            matrix(c), matrix(share + c), (((0,), (0,)), ((), ())), preferred_element_type=jnp.float32
        )
        for t in range(tiles):
            tri_ref[pl.ds((t * share + c) * loops * pad, loops * pad), :] = product[:, t * 128 : (t + 1) * 128]

    @pl.loop(0, rows)
    def pack(r):
        begin = r * local_rows
        begin = (begin // local_cols) * pad + begin % local_cols
        for l in range(loops):
            first, last = l * pad // 128, -(-(l * pad + local_cols) // 128)
            line = []
            for k in range(local_rows):
                here = [
                    tri_ref[pl.ds(t * share * loops * pad + begin + k, share, stride=loops * pad), :]
                    for t in range(first, last)
                ]
                offset = l * pad - first * 128
                line.append(jnp.concatenate(here, axis=1)[:, offset : offset + local_cols])
            out_ref[r * loops + l] = jnp.concatenate(line, axis=1).astype(jnp.bfloat16)


def line_triangle_kernel(inner, loops, local_rows, local_cols, in_ref, shifts_ref, returns_ref, out_ref, sides_ref, tri_ref):
    both = in_ref.shape[1]
    share = both // 2
    depth = inner * local_rows
    pairs = loops // 2
    group = local_cols // local_rows
    height = depth + 8
    block = loops * local_rows + 8
    lane = lax.broadcasted_iota(jnp.int32, (inner * both, 128), 1)

    blocks = [jnp.concatenate([in_ref[r * loops + l] for r in range(inner)], axis=0) for l in range(loops)]
    for n, offset in enumerate(line_offsets(local_rows, local_cols)):
        stack, target = [], []
        for pair in range(pairs):
            for k in range(local_rows):
                u = k * local_cols // 128
                if k * local_cols % 128 != offset:
                    continue
                line = []
                for side in blocks[2 * pair : 2 * pair + 2]:
                    tile = side[:, u * 128 : (u + 1) * 128]
                    if offset + local_cols > 128:
                        tile = jnp.where(lane >= offset, tile, side[:, (u + 1) * 128 : (u + 2) * 128])
                    line.append(tile)
                stack.append(jnp.concatenate(line, axis=1))
                target.append(pair * both * height + k)
        lines = jnp.dot(jnp.concatenate(stack, axis=0), shifts_ref[n], preferred_element_type=jnp.float32)
        for m, place in enumerate(target):
            for r in range(inner):
                for part in range(0, both, 8):
                    first = (m * inner + r) * both + part
                    target_rows = pl.ds(place + part * height + r * local_rows, 8, stride=height)
                    sides_ref[target_rows, :] = lines[first : first + 8]

    def matrix(index):
        return jnp.concatenate(
            [sides_ref[pl.ds((t * both + index) * height, depth), :] for t in range(pairs)], axis=1
        ).astype(jnp.bfloat16)

    for c in range(share):
        product = lax.dot_general(
            matrix(c), matrix(share + c), (((0,), (0,)), ((), ())), preferred_element_type=jnp.float32
        )
        for t in range(pairs):
            for h in range(group):
                for l in range(loops):
                    place = ((t * group + h) * share + c) * block + l * local_rows
                    first = l * 64 + h * local_rows
                    tri_ref[place : place + local_rows, :] = product[
                        first : first + local_rows, t * 128 : (t + 1) * 128
                    ]

    members = group * share
    period = math.lcm(local_cols, 128) // local_cols
    tiles = line_tiles(local_cols)
    for t in range(pairs):

        def tri_line(l, k):
            parts = [
                tri_ref[pl.ds((t * members + part) * block + l * local_rows + k, 8, stride=block), :]
                for part in range(0, members, 8)
            ]
            return jnp.concatenate(parts, axis=0).astype(jnp.bfloat16)

        begin = 0
        for u, (first, last) in enumerate(tiles):
            stack = [
                jnp.concatenate([tri_line(l, turn + k) for k in range(first, last + 1)], axis=1)
                for l in range(loops)
                for turn in range(0, local_rows, period)
            ]
            end = begin + (last + 1 - first) * 128
            lanes = jnp.dot(
                jnp.concatenate(stack, axis=0), returns_ref[begin:end, :], preferred_element_type=jnp.float32
            ).astype(jnp.bfloat16)
            begin = end
            for l in range(loops):
                for turn in range(local_rows // period):
                    place = (turn * len(tiles) + u) * 128
                    for h in range(group):
                        row = ((l * (local_rows // period) + turn) * group + h) * share
                        for side in range(2):
                            out_ref[(l * group + h) * loops + 2 * t + side, :, place : place + 128] = lanes[
                                row : row + share, side * 128 : (side + 1) * 128
                            ]


def make_sides(owners, local_rows, local_cols, *given):
    places, channels = given[0].shape
    wide = given[1].shape[1]
    hidden = wide // 4
    returns = sum(last + 1 - first for first, last in line_tiles(local_cols))
    return pl.pallas_call(
        functools.partial(sides_kernel, owners, local_rows, local_cols),
        out_shape=(
            jax.ShapeDtypeStruct((wide // 2, places), jnp.bfloat16),
            jax.ShapeDtypeStruct((channels, places), jnp.float32),
            jax.ShapeDtypeStruct((2, hidden, 128), jnp.float32),
            jax.ShapeDtypeStruct((channels, hidden), jnp.bfloat16),
            jax.ShapeDtypeStruct((len(line_offsets(local_rows, local_cols)), 256, 128), jnp.bfloat16),
            jax.ShapeDtypeStruct((returns * 128, 256), jnp.bfloat16),
        ),
        in_specs=[in_hbm] * len(given),
        out_specs=[in_vmem] * 6,
        scratch_shapes=[pltpu.VMEM(x.shape, x.dtype) for x in given] + [pltpu.SemaphoreType.DMA((len(given),))],
        compiler_params=pltpu.CompilerParams(vmem_limit_bytes=vmem_bytes),
        name="sides",
    )(*[pltpu.with_memory_space_constraint(x, pltpu.HBM) for x in given])


def update_kernel(tri_ref, gating_ref, columns_ref, w_ref, out_ref):
    values = tri_ref[0].astype(jnp.float32)
    for half in range(1, tri_ref.shape[0]):
        values += tri_ref[half].astype(jnp.float32)
    center = values - jnp.mean(values, axis=0, keepdims=True)
    spread = jnp.mean(center * center, axis=0, keepdims=True)
    mixed = center * lax.rsqrt(spread + epsilon) * columns_ref[0][:, :1] + columns_ref[1][:, :1]
    outgoing = jnp.dot(w_ref[...], mixed.astype(jnp.bfloat16), preferred_element_type=jnp.float32)
    out_ref[...] = (gating_ref[...] * outgoing).T.astype(jnp.bfloat16)


def make_update(triangle, gating, columns, w_out_t):
    channels, places = gating.shape
    return pl.pallas_call(
        update_kernel,
        out_shape=jax.ShapeDtypeStruct((places, channels), jnp.bfloat16),
        in_specs=[in_vmem] * 4,
        out_specs=in_vmem,
        compiler_params=pltpu.CompilerParams(vmem_limit_bytes=vmem_bytes),
        name="update",
    )(triangle, gating, columns, w_out_t)


def make_triangle(sides, shifts, returns, rows, inner, loops, local_rows, local_cols):
    owners, both, places = sides.shape
    share = both // 2
    operands = [sides]
    if in_lines(rows, loops, share, local_rows, local_cols):
        operands += [shifts, returns]
        kernel = functools.partial(line_triangle_kernel, inner, loops, local_rows, local_cols)
        sides_rows = (loops // 2 * both + 1) * (inner * local_rows + 8)
        tri_rows = (loops // 2 * share * (local_cols // local_rows) + 1) * (loops * local_rows + 8)
    else:
        pad = 64 if local_cols <= 64 and loops % 2 == 0 else -(-local_cols // 128) * 128
        kernel = functools.partial(triangle_kernel, rows, inner, loops, local_rows, local_cols, pad)
        sides_rows = loops * pad // 128 * both * inner * local_rows
        tri_rows = loops * pad // 128 * share * loops * pad
    return pl.pallas_call(
        kernel,
        out_shape=jax.ShapeDtypeStruct((rows * loops, share, places), jnp.bfloat16),
        in_specs=[in_vmem] * len(operands),
        out_specs=in_vmem,
        scratch_shapes=[
            pltpu.VMEM((sides_rows, 128), jnp.float32),
            pltpu.VMEM((tri_rows, 128), jnp.float32),
        ],
        compiler_params=pltpu.CompilerParams(vmem_limit_bytes=vmem_bytes),
        name="triangle",
    )(*operands)


def on_device(halves, inner, loops, pair, ln_in_gain, ln_in_bias, w_proj, w_gate, ln_out_gain, ln_out_bias, w_out):
    local_rows, local_cols, channels = pair.shape
    hidden = w_out.shape[0]
    owners = inner * loops
    share = hidden // owners
    places = local_rows * local_cols

    sides, gating, columns, w_out_t, shifts, returns = make_sides(
        owners,
        local_rows,
        local_cols,
        pair.reshape(places, channels),
        w_proj,
        w_gate,
        ln_in_gain[None],
        ln_in_bias[None],
        ln_out_gain[None],
        ln_out_bias[None],
        w_out,
    )
    sides = lax.all_to_all(
        sides.reshape(owners, 2 * share, places), ("inner", "loop"), split_axis=0, concat_axis=0
    )
    triangle = make_triangle(
        sides, shifts, returns, halves * inner, inner, loops, local_rows, local_cols
    )
    triangle = lax.all_to_all(triangle, ("half", "inner", "loop"), split_axis=0, concat_axis=0)
    update = make_update(triangle.reshape(halves, hidden, places), gating, columns, w_out_t)
    return update.reshape(local_rows, local_cols, channels)


def solution(mesh):
    rows, loops = mesh.shape["row"], mesh.shape["loop"]
    halves = 2 if rows % 2 == 0 else 1
    inner = rows // halves
    split = Mesh(mesh.devices.reshape(halves, inner, loops), ("half", "inner", "loop"))
    placed = P(("half", "inner"), "loop", None)
    return jax.shard_map(
        lambda *arrays: on_device(halves, inner, loops, *arrays),
        mesh=split,
        in_specs=(placed, P(), P(), P(), P(), P(), P(), P()),
        out_specs=placed,
        check_vma=False,
    )
```

```python
import functools
import math

import jax
import jax.numpy as jnp
from jax import lax
from jax.experimental import pallas as pl
from jax.experimental.pallas import tpu as pltpu
from jax.sharding import Mesh
from jax.sharding import PartitionSpec as P

epsilon = 1e-05
in_vmem = pl.BlockSpec(memory_space=pltpu.VMEM)
in_hbm = pl.BlockSpec(memory_space=pltpu.HBM)
vmem_bytes = 48 * 2**20


def line_groups(local_cols):
    groups = []
    for k in range(math.lcm(local_cols, 128) // local_cols):
        tile, offset = divmod(k * local_cols, 128)
        over = offset + local_cols > 128
        if over or not groups or groups[-1][0] != tile:
            groups.append((tile, k, 1))
        else:
            groups[-1] = (tile, groups[-1][1], groups[-1][2] + 1)
    return groups


def line_tiles(local_cols):
    tiles = math.lcm(local_cols, 128) // 128
    return [(u * 128 // local_cols, ((u + 1) * 128 - 1) // local_cols) for u in range(tiles)]


def in_lines(rows, loops, share, local_rows, local_cols):
    return (
        local_cols <= 64
        and local_cols % local_rows == 0
        and local_rows % 8 == 0
        and local_rows % (math.lcm(local_cols, 128) // local_cols) == 0
        and loops % 2 == 0
        and rows * local_rows == loops * local_cols
        and share % 8 == 0
    )


def sides_kernel(owners, local_cols, *refs):
    given, results, held, sems = refs[:8], refs[8:14], refs[14:22], refs[22]
    out_ref, gating_ref, columns_ref, w_out_t_ref, shifts_ref, returns_ref = results
    copies = [pltpu.make_async_copy(*ends, sems.at[n]) for n, ends in enumerate(zip(given, held))]
    for copy in copies:
        copy.start()
    pair_ref, w_proj_ref, w_gate_ref, in_gain_ref, in_bias_ref, out_gain_ref, out_bias_ref, w_out_ref = held
    wide = w_proj_ref.shape[1]
    half, hidden = wide // 2, wide // 4
    share = hidden // owners

    row = lax.broadcasted_iota(jnp.int32, (1, wide), 1)
    value, row = row // half, row % half
    owner, row = row // (2 * share), row % (2 * share)
    column = ((row // share) * 2 + value) * hidden + owner * share + row % share
    source = lax.broadcasted_iota(jnp.int32, (wide, wide), 0)
    pick = jnp.where(source == column, 1.0, 0.0).astype(jnp.bfloat16)

    source = lax.broadcasted_iota(jnp.int32, (256, 128), 0)
    lane = lax.broadcasted_iota(jnp.int32, (256, 128), 1)
    for k in range(shifts_ref.shape[1] // 128):
        wanted = ((lane & 63) + k * local_cols % 128) & 127
        wanted = jnp.where(lane >= 64, wanted + 128, wanted)
        picked = (source == wanted) & ((lane & 63) < local_cols)
        shifts_ref[:, k * 128 : (k + 1) * 128] = jnp.where(picked, 1.0, 0.0).astype(jnp.bfloat16)

    source = lax.broadcasted_iota(jnp.int32, (128, 256), 0)
    lane = lax.broadcasted_iota(jnp.int32, (128, 256), 1)
    begin = 0
    for u, (first, last) in enumerate(line_tiles(local_cols)):
        for k in range(first, last + 1):
            inside = (lane & 127) + (u * 128 - k * local_cols)
            wanted = jnp.where(lane >= 128, inside + 64, inside)
            picked = (source == wanted) & (inside >= 0) & (inside < local_cols)
            returns_ref[begin : begin + 128, :] = jnp.where(picked, 1.0, 0.0).astype(jnp.bfloat16)
            begin += 128

    for copy in copies:
        copy.wait()
    weights = jnp.dot(w_proj_ref[...], pick, preferred_element_type=jnp.float32).T.astype(jnp.bfloat16)
    weights = jnp.concatenate([weights, w_gate_ref[...].astype(jnp.float32).T.astype(jnp.bfloat16)], axis=0)
    values = pair_ref[...].astype(jnp.float32)
    center = values - jnp.mean(values, axis=-1, keepdims=True)
    spread = jnp.mean(center * center, axis=-1, keepdims=True)
    normed = center * lax.rsqrt(spread + epsilon) * in_gain_ref[...] + in_bias_ref[...]
    projected = lax.dot_general(
        weights, normed.astype(jnp.bfloat16), (((1,), (1,)), ((), ())), preferred_element_type=jnp.float32
    )
    sides = jax.nn.sigmoid(projected[:half]) * projected[half:wide]
    out_ref[...] = sides.astype(jnp.bfloat16)
    gating_ref[...] = jax.nn.sigmoid(projected[wide:])
    columns_ref[0] = jnp.broadcast_to(out_gain_ref[...], (128, hidden)).T
    columns_ref[1] = jnp.broadcast_to(out_bias_ref[...], (128, hidden)).T
    w_out_t_ref[...] = w_out_ref[...].astype(jnp.float32).T.astype(jnp.bfloat16)


def triangle_kernel(rows, inner, loops, local_rows, local_cols, pad, in_ref, out_ref, sides_ref, tri_ref):
    both = in_ref.shape[1]
    share = both // 2
    depth = inner * local_rows
    tiles = loops * pad // 128
    blank = jnp.zeros((both, pad - local_cols), jnp.float32)

    @pl.loop(0, inner)
    def unpack(r):
        blocks = [in_ref[r * loops + l].astype(jnp.float32) for l in range(loops)]
        for k in range(local_rows):
            line = []
            for block in blocks:
                line.append(block[:, k * local_cols : (k + 1) * local_cols])
                if pad > local_cols:
                    line.append(blank)
            line = jnp.concatenate(line, axis=1)
            for t in range(tiles):
                place = pl.ds(t * both * depth + r * local_rows + k, both, stride=depth)
                sides_ref[place, :] = line[:, t * 128 : (t + 1) * 128]

    def matrix(index):
        return jnp.concatenate(
            [sides_ref[pl.ds((t * both + index) * depth, depth), :] for t in range(tiles)], axis=1
        ).astype(jnp.bfloat16)

    for c in range(share):
        product = lax.dot_general(
            matrix(c), matrix(share + c), (((0,), (0,)), ((), ())), preferred_element_type=jnp.float32
        )
        for t in range(tiles):
            tri_ref[pl.ds((t * share + c) * loops * pad, loops * pad), :] = product[:, t * 128 : (t + 1) * 128]

    @pl.loop(0, rows)
    def pack(r):
        begin = r * local_rows
        begin = (begin // local_cols) * pad + begin % local_cols
        for l in range(loops):
            first, last = l * pad // 128, -(-(l * pad + local_cols) // 128)
            line = []
            for k in range(local_rows):
                here = [
                    tri_ref[pl.ds(t * share * loops * pad + begin + k, share, stride=loops * pad), :]
                    for t in range(first, last)
                ]
                offset = l * pad - first * 128
                line.append(jnp.concatenate(here, axis=1)[:, offset : offset + local_cols])
            out_ref[r * loops + l] = jnp.concatenate(line, axis=1).astype(jnp.bfloat16)


def line_triangle_kernel(inner, loops, local_rows, local_cols, in_ref, shifts_ref, returns_ref, out_ref, sides_ref, tri_ref):
    both = in_ref.shape[1]
    share = both // 2
    depth = inner * local_rows
    pairs = loops // 2
    group = local_cols // local_rows
    height = depth + 8
    block = loops * local_rows + 8
    lane = lax.broadcasted_iota(jnp.int32, (inner * both, 128), 1)

    blocks = [jnp.concatenate([in_ref[r * loops + l] for r in range(inner)], axis=0) for l in range(loops)]
    period = math.lcm(local_cols, 128) // local_cols
    tiles = line_tiles(local_cols)
    for u, k, count in line_groups(local_cols):
        offset = k * local_cols % 128
        stack, target = [], []
        for pair in range(pairs):
            for turn in range(local_rows // period):
                line = []
                for side in blocks[2 * pair : 2 * pair + 2]:
                    at = (turn * len(tiles) + u) * 128
                    tile = side[:, at : at + 128]
                    if offset + local_cols > 128:
                        tile = jnp.where(lane >= offset, tile, side[:, at + 128 : at + 256])
                    line.append(tile)
                stack.append(jnp.concatenate(line, axis=1))
                target.append(pair * both * height + turn * period + k)
        lines = jnp.dot(
            jnp.concatenate(stack, axis=0),
            shifts_ref[:, k * 128 : (k + count) * 128],
            preferred_element_type=jnp.float32,
        )
        for m, place in enumerate(target):
            for r in range(inner):
                for part in range(0, both, 8):
                    first = (m * inner + r) * both + part
                    for n in range(count):
                        target_rows = pl.ds(place + part * height + r * local_rows + n, 8, stride=height)
                        sides_ref[target_rows, :] = lines[first : first + 8, n * 128 : (n + 1) * 128]

    def matrix(index):
        return jnp.concatenate(
            [sides_ref[pl.ds((t * both + index) * height, depth), :] for t in range(pairs)], axis=1
        ).astype(jnp.bfloat16)

    for c in range(share):
        product = lax.dot_general(
            matrix(c), matrix(share + c), (((0,), (0,)), ((), ())), preferred_element_type=jnp.float32
        )
        for t in range(pairs):
            for h in range(group):
                for l in range(loops):
                    place = ((t * group + h) * share + c) * block + l * local_rows
                    first = l * 64 + h * local_rows
                    tri_ref[place : place + local_rows, :] = product[
                        first : first + local_rows, t * 128 : (t + 1) * 128
                    ]

    members = group * share
    for t in range(pairs):

        def tri_line(l, k):
            parts = [
                tri_ref[pl.ds((t * members + part) * block + l * local_rows + k, 8, stride=block), :]
                for part in range(0, members, 8)
            ]
            return jnp.concatenate(parts, axis=0).astype(jnp.bfloat16)

        begin = 0
        for u, (first, last) in enumerate(tiles):
            stack = [
                jnp.concatenate([tri_line(l, turn + k) for k in range(first, last + 1)], axis=1)
                for l in range(loops)
                for turn in range(0, local_rows, period)
            ]
            end = begin + (last + 1 - first) * 128
            lanes = jnp.dot(
                jnp.concatenate(stack, axis=0), returns_ref[begin:end, :], preferred_element_type=jnp.float32
            ).astype(jnp.bfloat16)
            begin = end
            for l in range(loops):
                for turn in range(local_rows // period):
                    place = (turn * len(tiles) + u) * 128
                    for h in range(group):
                        row = ((l * (local_rows // period) + turn) * group + h) * share
                        for side in range(2):
                            out_ref[(l * group + h) * loops + 2 * t + side, :, place : place + 128] = lanes[
                                row : row + share, side * 128 : (side + 1) * 128
                            ]


def make_sides(owners, local_cols, *given):
    places, channels = given[0].shape
    wide = given[1].shape[1]
    hidden = wide // 4
    returns = sum(last + 1 - first for first, last in line_tiles(local_cols))
    return pl.pallas_call(
        functools.partial(sides_kernel, owners, local_cols),
        out_shape=(
            jax.ShapeDtypeStruct((wide // 2, places), jnp.bfloat16),
            jax.ShapeDtypeStruct((channels, places), jnp.float32),
            jax.ShapeDtypeStruct((2, hidden, 128), jnp.float32),
            jax.ShapeDtypeStruct((channels, hidden), jnp.bfloat16),
            jax.ShapeDtypeStruct((256, math.lcm(local_cols, 128) // local_cols * 128), jnp.bfloat16),
            jax.ShapeDtypeStruct((returns * 128, 256), jnp.bfloat16),
        ),
        in_specs=[in_hbm] * len(given),
        out_specs=[in_vmem] * 6,
        scratch_shapes=[pltpu.VMEM(x.shape, x.dtype) for x in given] + [pltpu.SemaphoreType.DMA((len(given),))],
        compiler_params=pltpu.CompilerParams(vmem_limit_bytes=vmem_bytes),
        name="sides",
    )(*[pltpu.with_memory_space_constraint(x, pltpu.HBM) for x in given])


def update_kernel(tri_ref, gating_ref, columns_ref, w_ref, out_ref):
    values = tri_ref[0].astype(jnp.float32)
    for half in range(1, tri_ref.shape[0]):
        values += tri_ref[half].astype(jnp.float32)
    center = values - jnp.mean(values, axis=0, keepdims=True)
    spread = jnp.mean(center * center, axis=0, keepdims=True)
    mixed = center * lax.rsqrt(spread + epsilon) * columns_ref[0][:, :1] + columns_ref[1][:, :1]
    outgoing = jnp.dot(w_ref[...], mixed.astype(jnp.bfloat16), preferred_element_type=jnp.float32)
    out_ref[...] = (gating_ref[...] * outgoing).T.astype(jnp.bfloat16)


def make_update(triangle, gating, columns, w_out_t):
    channels, places = gating.shape
    return pl.pallas_call(
        update_kernel,
        out_shape=jax.ShapeDtypeStruct((places, channels), jnp.bfloat16),
        in_specs=[in_vmem] * 4,
        out_specs=in_vmem,
        compiler_params=pltpu.CompilerParams(vmem_limit_bytes=vmem_bytes),
        name="update",
    )(triangle, gating, columns, w_out_t)


def make_triangle(sides, shifts, returns, rows, inner, loops, local_rows, local_cols):
    owners, both, places = sides.shape
    share = both // 2
    operands = [sides]
    if in_lines(rows, loops, share, local_rows, local_cols):
        operands += [shifts, returns]
        kernel = functools.partial(line_triangle_kernel, inner, loops, local_rows, local_cols)
        sides_rows = (loops // 2 * both + 1) * (inner * local_rows + 8)
        tri_rows = (loops // 2 * share * (local_cols // local_rows) + 1) * (loops * local_rows + 8)
    else:
        pad = 64 if local_cols <= 64 and loops % 2 == 0 else -(-local_cols // 128) * 128
        kernel = functools.partial(triangle_kernel, rows, inner, loops, local_rows, local_cols, pad)
        sides_rows = loops * pad // 128 * both * inner * local_rows
        tri_rows = loops * pad // 128 * share * loops * pad
    return pl.pallas_call(
        kernel,
        out_shape=jax.ShapeDtypeStruct((rows * loops, share, places), jnp.bfloat16),
        in_specs=[in_vmem] * len(operands),
        out_specs=in_vmem,
        scratch_shapes=[
            pltpu.VMEM((sides_rows, 128), jnp.float32),
            pltpu.VMEM((tri_rows, 128), jnp.float32),
        ],
        compiler_params=pltpu.CompilerParams(vmem_limit_bytes=vmem_bytes),
        name="triangle",
    )(*operands)


def on_device(halves, inner, loops, pair, ln_in_gain, ln_in_bias, w_proj, w_gate, ln_out_gain, ln_out_bias, w_out):
    local_rows, local_cols, channels = pair.shape
    hidden = w_out.shape[0]
    owners = inner * loops
    share = hidden // owners
    places = local_rows * local_cols

    sides, gating, columns, w_out_t, shifts, returns = make_sides(
        owners,
        local_cols,
        pair.reshape(places, channels),
        w_proj,
        w_gate,
        ln_in_gain[None],
        ln_in_bias[None],
        ln_out_gain[None],
        ln_out_bias[None],
        w_out,
    )
    sides = lax.all_to_all(
        sides.reshape(owners, 2 * share, places), ("inner", "loop"), split_axis=0, concat_axis=0
    )
    triangle = make_triangle(
        sides, shifts, returns, halves * inner, inner, loops, local_rows, local_cols
    )
    triangle = lax.all_to_all(triangle, ("half", "inner", "loop"), split_axis=0, concat_axis=0)
    update = make_update(triangle.reshape(halves, hidden, places), gating, columns, w_out_t)
    return update.reshape(local_rows, local_cols, channels)


def solution(mesh):
    rows, loops = mesh.shape["row"], mesh.shape["loop"]
    halves = 2 if rows % 2 == 0 else 1
    inner = rows // halves
    split = Mesh(mesh.devices.reshape(halves, inner, loops), ("half", "inner", "loop"))
    placed = P(("half", "inner"), "loop", None)
    return jax.shard_map(
        lambda *arrays: on_device(halves, inner, loops, *arrays),
        mesh=split,
        in_specs=(placed, P(), P(), P(), P(), P(), P(), P()),
        out_specs=placed,
        check_vma=False,
    )
```

```python
import functools
import math

import jax
import jax.numpy as jnp
from jax import lax
from jax.experimental import pallas as pl
from jax.experimental.pallas import tpu as pltpu
from jax.sharding import Mesh
from jax.sharding import PartitionSpec as P

epsilon = 1e-05
in_vmem = pl.BlockSpec(memory_space=pltpu.VMEM)
in_hbm = pl.BlockSpec(memory_space=pltpu.HBM)
vmem_bytes = 48 * 2**20


def line_groups(local_cols):
    groups = []
    for k in range(math.lcm(local_cols, 128) // local_cols):
        tile, offset = divmod(k * local_cols, 128)
        over = offset + local_cols > 128
        if over or not groups or groups[-1][0] != tile:
            groups.append((tile, k, 1))
        else:
            groups[-1] = (tile, groups[-1][1], groups[-1][2] + 1)
    return groups


def line_tiles(local_cols):
    tiles = math.lcm(local_cols, 128) // 128
    return [(u * 128 // local_cols, ((u + 1) * 128 - 1) // local_cols) for u in range(tiles)]


def in_lines(rows, loops, share, local_rows, local_cols):
    return (
        local_cols <= 64
        and local_cols % local_rows == 0
        and local_rows % 8 == 0
        and local_rows % (math.lcm(local_cols, 128) // local_cols) == 0
        and loops % 2 == 0
        and rows * local_rows == loops * local_cols
        and share % 8 == 0
    )


def sides_kernel(owners, local_cols, *refs):
    given, results, held, sems = refs[:8], refs[8:14], refs[14:22], refs[22]
    out_ref, gating_ref, columns_ref, w_out_t_ref, shifts_ref, returns_ref = results
    copies = [pltpu.make_async_copy(*ends, sems.at[n]) for n, ends in enumerate(zip(given, held))]
    for copy in copies:
        copy.start()
    pair_ref, w_proj_ref, w_gate_ref, in_gain_ref, in_bias_ref, out_gain_ref, out_bias_ref, w_out_ref = held
    hidden = w_proj_ref.shape[1] // 4
    share = hidden // owners

    source = lax.broadcasted_iota(jnp.int32, (256, 128), 0)
    lane = lax.broadcasted_iota(jnp.int32, (256, 128), 1)
    for k in range(shifts_ref.shape[1] // 128):
        wanted = ((lane & 63) + k * local_cols % 128) & 127
        wanted = jnp.where(lane >= 64, wanted + 128, wanted)
        picked = (source == wanted) & ((lane & 63) < local_cols)
        shifts_ref[:, k * 128 : (k + 1) * 128] = jnp.where(picked, 1.0, 0.0).astype(jnp.bfloat16)

    source = lax.broadcasted_iota(jnp.int32, (128, 256), 0)
    lane = lax.broadcasted_iota(jnp.int32, (128, 256), 1)
    begin = 0
    for u, (first, last) in enumerate(line_tiles(local_cols)):
        for k in range(first, last + 1):
            inside = (lane & 127) + (u * 128 - k * local_cols)
            wanted = jnp.where(lane >= 128, inside + 64, inside)
            picked = (source == wanted) & (inside >= 0) & (inside < local_cols)
            returns_ref[begin : begin + 128, :] = jnp.where(picked, 1.0, 0.0).astype(jnp.bfloat16)
            begin += 128

    for copy in copies:
        copy.wait()
    values = pair_ref[...].astype(jnp.float32)
    center = values - jnp.mean(values, axis=-1, keepdims=True)
    spread = jnp.mean(center * center, axis=-1, keepdims=True)
    normed = center * lax.rsqrt(spread + epsilon) * in_gain_ref[...] + in_bias_ref[...]
    normed = normed.astype(jnp.bfloat16)
    projected, gate = [
        lax.dot_general(weights[...], normed, (((0,), (1,)), ((), ())), preferred_element_type=jnp.float32)
        for weights in (w_proj_ref, w_gate_ref)
    ]
    left_gate, left, right_gate, right = [projected[n * hidden : (n + 1) * hidden] for n in range(4)]
    left = jax.nn.sigmoid(left_gate) * left
    right = jax.nn.sigmoid(right_gate) * right
    sides = [side[at : at + share] for at in range(0, hidden, share) for side in (left, right)]
    out_ref[...] = jnp.concatenate(sides, axis=0).astype(jnp.bfloat16)
    gating_ref[...] = jax.nn.sigmoid(gate)
    columns_ref[0] = jnp.broadcast_to(out_gain_ref[...], (128, hidden)).T
    columns_ref[1] = jnp.broadcast_to(out_bias_ref[...], (128, hidden)).T
    w_out_t_ref[...] = w_out_ref[...].astype(jnp.float32).T.astype(jnp.bfloat16)


def triangle_kernel(rows, inner, loops, local_rows, local_cols, pad, in_ref, out_ref, sides_ref, tri_ref):
    both = in_ref.shape[1]
    share = both // 2
    depth = inner * local_rows
    tiles = loops * pad // 128
    blank = jnp.zeros((both, pad - local_cols), jnp.float32)

    @pl.loop(0, inner)
    def unpack(r):
        blocks = [in_ref[r * loops + l].astype(jnp.float32) for l in range(loops)]
        for k in range(local_rows):
            line = []
            for block in blocks:
                line.append(block[:, k * local_cols : (k + 1) * local_cols])
                if pad > local_cols:
                    line.append(blank)
            line = jnp.concatenate(line, axis=1)
            for t in range(tiles):
                place = pl.ds(t * both * depth + r * local_rows + k, both, stride=depth)
                sides_ref[place, :] = line[:, t * 128 : (t + 1) * 128]

    def matrix(index):
        return jnp.concatenate(
            [sides_ref[pl.ds((t * both + index) * depth, depth), :] for t in range(tiles)], axis=1
        ).astype(jnp.bfloat16)

    for c in range(share):
        product = lax.dot_general(
            matrix(c), matrix(share + c), (((0,), (0,)), ((), ())), preferred_element_type=jnp.float32
        )
        for t in range(tiles):
            tri_ref[pl.ds((t * share + c) * loops * pad, loops * pad), :] = product[:, t * 128 : (t + 1) * 128]

    @pl.loop(0, rows)
    def pack(r):
        begin = r * local_rows
        begin = (begin // local_cols) * pad + begin % local_cols
        for l in range(loops):
            first, last = l * pad // 128, -(-(l * pad + local_cols) // 128)
            line = []
            for k in range(local_rows):
                here = [
                    tri_ref[pl.ds(t * share * loops * pad + begin + k, share, stride=loops * pad), :]
                    for t in range(first, last)
                ]
                offset = l * pad - first * 128
                line.append(jnp.concatenate(here, axis=1)[:, offset : offset + local_cols])
            out_ref[r * loops + l] = jnp.concatenate(line, axis=1).astype(jnp.bfloat16)


def line_triangle_kernel(inner, loops, local_rows, local_cols, in_ref, shifts_ref, returns_ref, out_ref, sides_ref, tri_ref):
    both = in_ref.shape[1]
    share = both // 2
    depth = inner * local_rows
    pairs = loops // 2
    group = local_cols // local_rows
    height = depth + 8
    block = loops * local_rows + 8
    lane = lax.broadcasted_iota(jnp.int32, (inner * both, 128), 1)

    blocks = [jnp.concatenate([in_ref[r * loops + l] for r in range(inner)], axis=0) for l in range(loops)]
    period = math.lcm(local_cols, 128) // local_cols
    tiles = line_tiles(local_cols)
    for u, k, count in line_groups(local_cols):
        offset = k * local_cols % 128
        stack, target = [], []
        for pair in range(pairs):
            for turn in range(local_rows // period):
                line = []
                for side in blocks[2 * pair : 2 * pair + 2]:
                    at = (turn * len(tiles) + u) * 128
                    tile = side[:, at : at + 128]
                    if offset + local_cols > 128:
                        tile = jnp.where(lane >= offset, tile, side[:, at + 128 : at + 256])
                    line.append(tile)
                stack.append(jnp.concatenate(line, axis=1))
                target.append(pair * both * height + turn * period + k)
        lines = jnp.dot(
            jnp.concatenate(stack, axis=0),
            shifts_ref[:, k * 128 : (k + count) * 128],
            preferred_element_type=jnp.float32,
        )
        for m, place in enumerate(target):
            for r in range(inner):
                for part in range(0, both, 8):
                    first = (m * inner + r) * both + part
                    for n in range(count):
                        target_rows = pl.ds(place + part * height + r * local_rows + n, 8, stride=height)
                        sides_ref[target_rows, :] = lines[first : first + 8, n * 128 : (n + 1) * 128]

    def matrix(index):
        return jnp.concatenate(
            [sides_ref[pl.ds((t * both + index) * height, depth), :] for t in range(pairs)], axis=1
        ).astype(jnp.bfloat16)

    for c in range(share):
        product = lax.dot_general(
            matrix(c), matrix(share + c), (((0,), (0,)), ((), ())), preferred_element_type=jnp.float32
        )
        for t in range(pairs):
            for h in range(group):
                for l in range(loops):
                    place = ((t * group + h) * share + c) * block + l * local_rows
                    first = l * 64 + h * local_rows
                    tri_ref[place : place + local_rows, :] = product[
                        first : first + local_rows, t * 128 : (t + 1) * 128
                    ]

    members = group * share
    for t in range(pairs):

        def tri_line(l, k):
            parts = [
                tri_ref[pl.ds((t * members + part) * block + l * local_rows + k, 8, stride=block), :]
                for part in range(0, members, 8)
            ]
            return jnp.concatenate(parts, axis=0).astype(jnp.bfloat16)

        begin = 0
        for u, (first, last) in enumerate(tiles):
            stack = [
                jnp.concatenate([tri_line(l, turn + k) for k in range(first, last + 1)], axis=1)
                for l in range(loops)
                for turn in range(0, local_rows, period)
            ]
            end = begin + (last + 1 - first) * 128
            lanes = jnp.dot(
                jnp.concatenate(stack, axis=0), returns_ref[begin:end, :], preferred_element_type=jnp.float32
            ).astype(jnp.bfloat16)
            begin = end
            for l in range(loops):
                for turn in range(local_rows // period):
                    place = (turn * len(tiles) + u) * 128
                    for h in range(group):
                        row = ((l * (local_rows // period) + turn) * group + h) * share
                        for side in range(2):
                            out_ref[(l * group + h) * loops + 2 * t + side, :, place : place + 128] = lanes[
                                row : row + share, side * 128 : (side + 1) * 128
                            ]


def make_sides(owners, local_cols, *given):
    places, channels = given[0].shape
    wide = given[1].shape[1]
    hidden = wide // 4
    returns = sum(last + 1 - first for first, last in line_tiles(local_cols))
    return pl.pallas_call(
        functools.partial(sides_kernel, owners, local_cols),
        out_shape=(
            jax.ShapeDtypeStruct((wide // 2, places), jnp.bfloat16),
            jax.ShapeDtypeStruct((channels, places), jnp.float32),
            jax.ShapeDtypeStruct((2, hidden, 128), jnp.float32),
            jax.ShapeDtypeStruct((channels, hidden), jnp.bfloat16),
            jax.ShapeDtypeStruct((256, math.lcm(local_cols, 128) // local_cols * 128), jnp.bfloat16),
            jax.ShapeDtypeStruct((returns * 128, 256), jnp.bfloat16),
        ),
        in_specs=[in_hbm] * len(given),
        out_specs=[in_vmem] * 6,
        scratch_shapes=[pltpu.VMEM(x.shape, x.dtype) for x in given] + [pltpu.SemaphoreType.DMA((len(given),))],
        compiler_params=pltpu.CompilerParams(vmem_limit_bytes=vmem_bytes),
        name="sides",
    )(*[pltpu.with_memory_space_constraint(x, pltpu.HBM) for x in given])


def update_kernel(tri_ref, gating_ref, columns_ref, w_ref, out_ref):
    values = tri_ref[0].astype(jnp.float32)
    for half in range(1, tri_ref.shape[0]):
        values += tri_ref[half].astype(jnp.float32)
    center = values - jnp.mean(values, axis=0, keepdims=True)
    spread = jnp.mean(center * center, axis=0, keepdims=True)
    mixed = center * lax.rsqrt(spread + epsilon) * columns_ref[0][:, :1] + columns_ref[1][:, :1]
    outgoing = jnp.dot(w_ref[...], mixed.astype(jnp.bfloat16), preferred_element_type=jnp.float32)
    out_ref[...] = (gating_ref[...] * outgoing).T.astype(jnp.bfloat16)


def make_update(triangle, gating, columns, w_out_t):
    channels, places = gating.shape
    return pl.pallas_call(
        update_kernel,
        out_shape=jax.ShapeDtypeStruct((places, channels), jnp.bfloat16),
        in_specs=[in_vmem] * 4,
        out_specs=in_vmem,
        compiler_params=pltpu.CompilerParams(vmem_limit_bytes=vmem_bytes),
        name="update",
    )(triangle, gating, columns, w_out_t)


def make_triangle(sides, shifts, returns, rows, inner, loops, local_rows, local_cols):
    owners, both, places = sides.shape
    share = both // 2
    operands = [sides]
    if in_lines(rows, loops, share, local_rows, local_cols):
        operands += [shifts, returns]
        kernel = functools.partial(line_triangle_kernel, inner, loops, local_rows, local_cols)
        sides_rows = (loops // 2 * both + 1) * (inner * local_rows + 8)
        tri_rows = (loops // 2 * share * (local_cols // local_rows) + 1) * (loops * local_rows + 8)
    else:
        pad = 64 if local_cols <= 64 and loops % 2 == 0 else -(-local_cols // 128) * 128
        kernel = functools.partial(triangle_kernel, rows, inner, loops, local_rows, local_cols, pad)
        sides_rows = loops * pad // 128 * both * inner * local_rows
        tri_rows = loops * pad // 128 * share * loops * pad
    return pl.pallas_call(
        kernel,
        out_shape=jax.ShapeDtypeStruct((rows * loops, share, places), jnp.bfloat16),
        in_specs=[in_vmem] * len(operands),
        out_specs=in_vmem,
        scratch_shapes=[
            pltpu.VMEM((sides_rows, 128), jnp.float32),
            pltpu.VMEM((tri_rows, 128), jnp.float32),
        ],
        compiler_params=pltpu.CompilerParams(vmem_limit_bytes=vmem_bytes),
        name="triangle",
    )(*operands)


def on_device(halves, inner, loops, pair, ln_in_gain, ln_in_bias, w_proj, w_gate, ln_out_gain, ln_out_bias, w_out):
    local_rows, local_cols, channels = pair.shape
    hidden = w_out.shape[0]
    owners = inner * loops
    share = hidden // owners
    places = local_rows * local_cols

    sides, gating, columns, w_out_t, shifts, returns = make_sides(
        owners,
        local_cols,
        pair.reshape(places, channels),
        w_proj,
        w_gate,
        ln_in_gain[None],
        ln_in_bias[None],
        ln_out_gain[None],
        ln_out_bias[None],
        w_out,
    )
    sides = lax.all_to_all(
        sides.reshape(owners, 2 * share, places), ("inner", "loop"), split_axis=0, concat_axis=0
    )
    triangle = make_triangle(
        sides, shifts, returns, halves * inner, inner, loops, local_rows, local_cols
    )
    triangle = lax.all_to_all(triangle, ("half", "inner", "loop"), split_axis=0, concat_axis=0)
    update = make_update(triangle.reshape(halves, hidden, places), gating, columns, w_out_t)
    return update.reshape(local_rows, local_cols, channels)


def solution(mesh):
    rows, loops = mesh.shape["row"], mesh.shape["loop"]
    halves = 2 if rows % 2 == 0 else 1
    inner = rows // halves
    split = Mesh(mesh.devices.reshape(halves, inner, loops), ("half", "inner", "loop"))
    placed = P(("half", "inner"), "loop", None)
    return jax.shard_map(
        lambda *arrays: on_device(halves, inner, loops, *arrays),
        mesh=split,
        in_specs=(placed, P(), P(), P(), P(), P(), P(), P()),
        out_specs=placed,
        check_vma=False,
    )
```

```python
import functools
import math

import jax
import jax.numpy as jnp
from jax import lax
from jax.experimental import pallas as pl
from jax.experimental.pallas import tpu as pltpu
from jax.sharding import Mesh
from jax.sharding import PartitionSpec as P

epsilon = 1e-05
in_vmem = pl.BlockSpec(memory_space=pltpu.VMEM)
in_hbm = pl.BlockSpec(memory_space=pltpu.HBM)
vmem_bytes = 48 * 2**20


def line_groups(local_cols):
    groups = []
    for k in range(math.lcm(local_cols, 128) // local_cols):
        tile, offset = divmod(k * local_cols, 128)
        over = offset + local_cols > 128
        if over or not groups or groups[-1][0] != tile:
            groups.append((tile, k, 1))
        else:
            groups[-1] = (tile, groups[-1][1], groups[-1][2] + 1)
    return groups


def line_tiles(local_cols):
    tiles = math.lcm(local_cols, 128) // 128
    return [(u * 128 // local_cols, ((u + 1) * 128 - 1) // local_cols) for u in range(tiles)]


def in_lines(rows, loops, share, local_rows, local_cols):
    return (
        local_cols <= 64
        and local_cols % local_rows == 0
        and local_rows % 8 == 0
        and local_rows % (math.lcm(local_cols, 128) // local_cols) == 0
        and loops % 2 == 0
        and rows * local_rows == loops * local_cols
        and share % 8 == 0
    )


def sides_kernel(owners, local_cols, *refs):
    given, results, held, sems = refs[:8], refs[8:14], refs[14:22], refs[22]
    out_ref, gating_ref, columns_ref, w_out_t_ref, shifts_ref, returns_ref = results
    copies = [pltpu.make_async_copy(*ends, sems.at[n]) for n, ends in enumerate(zip(given, held))]
    for copy in copies:
        copy.start()
    pair_ref, w_proj_ref, w_gate_ref, in_gain_ref, in_bias_ref, out_gain_ref, out_bias_ref, w_out_ref = held
    hidden = w_proj_ref.shape[1] // 4
    share = hidden // owners

    source = lax.broadcasted_iota(jnp.int32, (256, 128), 0)
    lane = lax.broadcasted_iota(jnp.int32, (256, 128), 1)
    for k in range(shifts_ref.shape[1] // 128):
        wanted = ((lane & 63) + k * local_cols % 128) & 127
        wanted = jnp.where(lane >= 64, wanted + 128, wanted)
        picked = (source == wanted) & ((lane & 63) < local_cols)
        shifts_ref[:, k * 128 : (k + 1) * 128] = jnp.where(picked, 1.0, 0.0).astype(jnp.bfloat16)

    source = lax.broadcasted_iota(jnp.int32, (128, 256), 0)
    lane = lax.broadcasted_iota(jnp.int32, (128, 256), 1)
    begin = 0
    for u, (first, last) in enumerate(line_tiles(local_cols)):
        for k in range(first, last + 1):
            inside = (lane & 127) + (u * 128 - k * local_cols)
            wanted = jnp.where(lane >= 128, inside + 64, inside)
            picked = (source == wanted) & (inside >= 0) & (inside < local_cols)
            returns_ref[begin : begin + 128, :] = jnp.where(picked, 1.0, 0.0).astype(jnp.bfloat16)
            begin += 128

    for copy in copies:
        copy.wait()
    values = pair_ref[...].astype(jnp.float32)
    center = values - jnp.mean(values, axis=-1, keepdims=True)
    spread = jnp.mean(center * center, axis=-1, keepdims=True)
    normed = center * lax.rsqrt(spread + epsilon) * in_gain_ref[...] + in_bias_ref[...]
    normed = normed.astype(jnp.bfloat16)
    projected, gate = [
        lax.dot_general(weights[...], normed, (((0,), (1,)), ((), ())), preferred_element_type=jnp.float32)
        for weights in (w_proj_ref, w_gate_ref)
    ]
    left_gate, left, right_gate, right = [projected[n * hidden : (n + 1) * hidden] for n in range(4)]
    left = jax.nn.sigmoid(left_gate) * left
    right = jax.nn.sigmoid(right_gate) * right
    sides = [side[at : at + share] for at in range(0, hidden, share) for side in (left, right)]
    out_ref[...] = jnp.concatenate(sides, axis=0).astype(jnp.bfloat16)
    gating_ref[...] = jax.nn.sigmoid(gate)
    columns_ref[0] = jnp.broadcast_to(out_gain_ref[...], (128, hidden)).T
    columns_ref[1] = jnp.broadcast_to(out_bias_ref[...], (128, hidden)).T
    w_out_t_ref[...] = w_out_ref[...].astype(jnp.float32).T.astype(jnp.bfloat16)


def triangle_kernel(rows, inner, loops, local_rows, local_cols, pad, in_ref, out_ref, sides_ref, tri_ref):
    both = in_ref.shape[1]
    share = both // 2
    depth = inner * local_rows
    tiles = loops * pad // 128
    blank = jnp.zeros((both, pad - local_cols), jnp.float32)

    @pl.loop(0, inner)
    def unpack(r):
        blocks = [in_ref[r * loops + l].astype(jnp.float32) for l in range(loops)]
        for k in range(local_rows):
            line = []
            for block in blocks:
                line.append(block[:, k * local_cols : (k + 1) * local_cols])
                if pad > local_cols:
                    line.append(blank)
            line = jnp.concatenate(line, axis=1)
            for t in range(tiles):
                place = pl.ds(t * both * depth + r * local_rows + k, both, stride=depth)
                sides_ref[place, :] = line[:, t * 128 : (t + 1) * 128]

    def matrix(index):
        return jnp.concatenate(
            [sides_ref[pl.ds((t * both + index) * depth, depth), :] for t in range(tiles)], axis=1
        ).astype(jnp.bfloat16)

    for c in range(share):
        product = lax.dot_general(
            matrix(c), matrix(share + c), (((0,), (0,)), ((), ())), preferred_element_type=jnp.float32
        )
        for t in range(tiles):
            tri_ref[pl.ds((t * share + c) * loops * pad, loops * pad), :] = product[:, t * 128 : (t + 1) * 128]

    @pl.loop(0, rows)
    def pack(r):
        begin = r * local_rows
        begin = (begin // local_cols) * pad + begin % local_cols
        for l in range(loops):
            first, last = l * pad // 128, -(-(l * pad + local_cols) // 128)
            line = []
            for k in range(local_rows):
                here = [
                    tri_ref[pl.ds(t * share * loops * pad + begin + k, share, stride=loops * pad), :]
                    for t in range(first, last)
                ]
                offset = l * pad - first * 128
                line.append(jnp.concatenate(here, axis=1)[:, offset : offset + local_cols])
            out_ref[r * loops + l] = jnp.concatenate(line, axis=1).astype(jnp.bfloat16)


def line_triangle_kernel(inner, loops, local_rows, local_cols, in_ref, shifts_ref, returns_ref, out_ref, sides_ref, *tri_refs):
    both = in_ref.shape[1]
    share = both // 2
    depth = inner * local_rows
    pairs = loops // 2
    group = local_cols // local_rows
    height = depth + 8
    block = loops * local_rows + 8
    lane = lax.broadcasted_iota(jnp.int32, (inner * both, 128), 1)

    blocks = [jnp.concatenate([in_ref[r * loops + l] for r in range(inner)], axis=0) for l in range(loops)]
    period = math.lcm(local_cols, 128) // local_cols
    tiles = line_tiles(local_cols)
    for u, k, count in line_groups(local_cols):
        offset = k * local_cols % 128
        stack, target = [], []
        for pair in range(pairs):
            for turn in range(local_rows // period):
                line = []
                for side in blocks[2 * pair : 2 * pair + 2]:
                    at = (turn * len(tiles) + u) * 128
                    tile = side[:, at : at + 128]
                    if offset + local_cols > 128:
                        tile = jnp.where(lane >= offset, tile, side[:, at + 128 : at + 256])
                    line.append(tile)
                stack.append(jnp.concatenate(line, axis=1))
                target.append(pair * both * height + turn * period + k)
        lines = jnp.dot(
            jnp.concatenate(stack, axis=0),
            shifts_ref[:, k * 128 : (k + count) * 128],
            preferred_element_type=jnp.float32,
        )
        for m, place in enumerate(target):
            for r in range(inner):
                for part in range(0, both, 8):
                    first = (m * inner + r) * both + part
                    for n in range(count):
                        target_rows = pl.ds(place + part * height + r * local_rows + n, 8, stride=height)
                        sides_ref[target_rows, :] = lines[first : first + 8, n * 128 : (n + 1) * 128]

    def matrix(index):
        return jnp.concatenate(
            [sides_ref[pl.ds((t * both + index) * height, depth), :] for t in range(pairs)], axis=1
        ).astype(jnp.bfloat16)

    for t in range(pairs):
        for c in range(share):
            right = sides_ref[pl.ds((t * both + share + c) * height, depth), :].astype(jnp.bfloat16)
            product = lax.dot_general(
                matrix(c), right, (((0,), (0,)), ((), ())), preferred_element_type=jnp.float32
            )
            for h in range(group):
                for l in range(loops):
                    place = (h * share + c) * block + l * local_rows
                    first = l * 64 + h * local_rows
                    tri_refs[t][place : place + local_rows, :] = product[first : first + local_rows, :]

    members = group * share
    for t in range(pairs):

        def tri_line(l, k):
            parts = [
                tri_refs[t][pl.ds(part * block + l * local_rows + k, 8, stride=block), :]
                for part in range(0, members, 8)
            ]
            return jnp.concatenate(parts, axis=0).astype(jnp.bfloat16)

        begin = 0
        for u, (first, last) in enumerate(tiles):
            stack = [
                jnp.concatenate([tri_line(l, turn + k) for k in range(first, last + 1)], axis=1)
                for l in range(loops)
                for turn in range(0, local_rows, period)
            ]
            end = begin + (last + 1 - first) * 128
            lanes = jnp.dot(
                jnp.concatenate(stack, axis=0), returns_ref[begin:end, :], preferred_element_type=jnp.float32
            ).astype(jnp.bfloat16)
            begin = end
            for l in range(loops):
                for turn in range(local_rows // period):
                    place = (turn * len(tiles) + u) * 128
                    for h in range(group):
                        row = ((l * (local_rows // period) + turn) * group + h) * share
                        for side in range(2):
                            out_ref[(l * group + h) * loops + 2 * t + side, :, place : place + 128] = lanes[
                                row : row + share, side * 128 : (side + 1) * 128
                            ]


def make_sides(owners, local_cols, *given):
    places, channels = given[0].shape
    wide = given[1].shape[1]
    hidden = wide // 4
    returns = sum(last + 1 - first for first, last in line_tiles(local_cols))
    return pl.pallas_call(
        functools.partial(sides_kernel, owners, local_cols),
        out_shape=(
            jax.ShapeDtypeStruct((wide // 2, places), jnp.bfloat16),
            jax.ShapeDtypeStruct((channels, places), jnp.float32),
            jax.ShapeDtypeStruct((2, hidden, 128), jnp.float32),
            jax.ShapeDtypeStruct((channels, hidden), jnp.bfloat16),
            jax.ShapeDtypeStruct((256, math.lcm(local_cols, 128) // local_cols * 128), jnp.bfloat16),
            jax.ShapeDtypeStruct((returns * 128, 256), jnp.bfloat16),
        ),
        in_specs=[in_hbm] * len(given),
        out_specs=[in_vmem] * 6,
        scratch_shapes=[pltpu.VMEM(x.shape, x.dtype) for x in given] + [pltpu.SemaphoreType.DMA((len(given),))],
        compiler_params=pltpu.CompilerParams(vmem_limit_bytes=vmem_bytes),
        name="sides",
    )(*[pltpu.with_memory_space_constraint(x, pltpu.HBM) for x in given])


def update_kernel(tri_ref, gating_ref, columns_ref, w_ref, out_ref):
    values = tri_ref[0].astype(jnp.float32)
    for half in range(1, tri_ref.shape[0]):
        values += tri_ref[half].astype(jnp.float32)
    center = values - jnp.mean(values, axis=0, keepdims=True)
    spread = jnp.mean(center * center, axis=0, keepdims=True)
    mixed = center * lax.rsqrt(spread + epsilon) * columns_ref[0][:, :1] + columns_ref[1][:, :1]
    outgoing = jnp.dot(w_ref[...], mixed.astype(jnp.bfloat16), preferred_element_type=jnp.float32)
    out_ref[...] = (gating_ref[...] * outgoing).T.astype(jnp.bfloat16)


def make_update(triangle, gating, columns, w_out_t):
    channels, places = gating.shape
    return pl.pallas_call(
        update_kernel,
        out_shape=jax.ShapeDtypeStruct((places, channels), jnp.bfloat16),
        in_specs=[in_vmem] * 4,
        out_specs=in_vmem,
        compiler_params=pltpu.CompilerParams(vmem_limit_bytes=vmem_bytes),
        name="update",
    )(triangle, gating, columns, w_out_t)


def make_triangle(sides, shifts, returns, rows, inner, loops, local_rows, local_cols):
    owners, both, places = sides.shape
    share = both // 2
    operands = [sides]
    if in_lines(rows, loops, share, local_rows, local_cols):
        operands += [shifts, returns]
        kernel = functools.partial(line_triangle_kernel, inner, loops, local_rows, local_cols)
        sides_rows = (loops // 2 * both + 1) * (inner * local_rows + 8)
        tri_rows = [(share * (local_cols // local_rows) + 1) * (loops * local_rows + 8)] * (loops // 2)
    else:
        pad = 64 if local_cols <= 64 and loops % 2 == 0 else -(-local_cols // 128) * 128
        kernel = functools.partial(triangle_kernel, rows, inner, loops, local_rows, local_cols, pad)
        sides_rows = loops * pad // 128 * both * inner * local_rows
        tri_rows = [loops * pad // 128 * share * loops * pad]
    return pl.pallas_call(
        kernel,
        out_shape=jax.ShapeDtypeStruct((rows * loops, share, places), jnp.bfloat16),
        in_specs=[in_vmem] * len(operands),
        out_specs=in_vmem,
        scratch_shapes=[pltpu.VMEM((n, 128), jnp.float32) for n in [sides_rows] + tri_rows],
        compiler_params=pltpu.CompilerParams(vmem_limit_bytes=vmem_bytes),
        name="triangle",
    )(*operands)


def on_device(halves, inner, loops, pair, ln_in_gain, ln_in_bias, w_proj, w_gate, ln_out_gain, ln_out_bias, w_out):
    local_rows, local_cols, channels = pair.shape
    hidden = w_out.shape[0]
    owners = inner * loops
    share = hidden // owners
    places = local_rows * local_cols

    sides, gating, columns, w_out_t, shifts, returns = make_sides(
        owners,
        local_cols,
        pair.reshape(places, channels),
        w_proj,
        w_gate,
        ln_in_gain[None],
        ln_in_bias[None],
        ln_out_gain[None],
        ln_out_bias[None],
        w_out,
    )
    sides = lax.all_to_all(
        sides.reshape(owners, 2 * share, places), ("inner", "loop"), split_axis=0, concat_axis=0
    )
    triangle = make_triangle(
        sides, shifts, returns, halves * inner, inner, loops, local_rows, local_cols
    )
    triangle = lax.all_to_all(triangle, ("half", "inner", "loop"), split_axis=0, concat_axis=0)
    update = make_update(triangle.reshape(halves, hidden, places), gating, columns, w_out_t)
    return update.reshape(local_rows, local_cols, channels)


def solution(mesh):
    rows, loops = mesh.shape["row"], mesh.shape["loop"]
    halves = 2 if rows % 2 == 0 else 1
    inner = rows // halves
    split = Mesh(mesh.devices.reshape(halves, inner, loops), ("half", "inner", "loop"))
    placed = P(("half", "inner"), "loop", None)
    return jax.shard_map(
        lambda *arrays: on_device(halves, inner, loops, *arrays),
        mesh=split,
        in_specs=(placed, P(), P(), P(), P(), P(), P(), P()),
        out_specs=placed,
        check_vma=False,
    )
```

```python
import functools
import math

import jax
import jax.numpy as jnp
from jax import lax
from jax.experimental import pallas as pl
from jax.experimental.pallas import tpu as pltpu
from jax.sharding import Mesh
from jax.sharding import PartitionSpec as P

epsilon = 1e-05
in_vmem = pl.BlockSpec(memory_space=pltpu.VMEM)
in_hbm = pl.BlockSpec(memory_space=pltpu.HBM)
vmem_bytes = 48 * 2**20


def line_groups(local_cols):
    groups = []
    for k in range(math.lcm(local_cols, 128) // local_cols):
        tile, offset = divmod(k * local_cols, 128)
        over = offset + local_cols > 128
        if over or not groups or groups[-1][0] != tile:
            groups.append((tile, k, 1))
        else:
            groups[-1] = (tile, groups[-1][1], groups[-1][2] + 1)
    return groups


def line_tiles(local_cols):
    tiles = math.lcm(local_cols, 128) // 128
    return [(u * 128 // local_cols, ((u + 1) * 128 - 1) // local_cols) for u in range(tiles)]


def in_lines(rows, loops, share, local_rows, local_cols):
    return (
        local_cols <= 64
        and local_cols % local_rows == 0
        and local_rows % 8 == 0
        and local_rows % (math.lcm(local_cols, 128) // local_cols) == 0
        and loops % 2 == 0
        and rows * local_rows == loops * local_cols
        and share % 8 == 0
    )


def sides_kernel(owners, local_cols, *refs):
    given, results, held, sems = refs[:8], refs[8:14], refs[14:22], refs[22]
    out_ref, gating_ref, columns_ref, w_out_t_ref, shifts_ref, returns_ref = results
    copies = [pltpu.make_async_copy(*ends, sems.at[n]) for n, ends in enumerate(zip(given, held))]
    for copy in copies:
        copy.start()
    pair_ref, w_proj_ref, w_gate_ref, in_gain_ref, in_bias_ref, out_gain_ref, out_bias_ref, w_out_ref = held
    hidden = w_proj_ref.shape[1] // 4
    share = hidden // owners

    source = lax.broadcasted_iota(jnp.int32, (256, 128), 0)
    lane = lax.broadcasted_iota(jnp.int32, (256, 128), 1)
    for k in range(shifts_ref.shape[1] // 128):
        wanted = ((lane & 63) + k * local_cols % 128) & 127
        wanted = jnp.where(lane >= 64, wanted + 128, wanted)
        picked = (source == wanted) & ((lane & 63) < local_cols)
        shifts_ref[:, k * 128 : (k + 1) * 128] = jnp.where(picked, 1.0, 0.0).astype(jnp.bfloat16)

    source = lax.broadcasted_iota(jnp.int32, (128, 256), 0)
    lane = lax.broadcasted_iota(jnp.int32, (128, 256), 1)
    begin = 0
    for u, (first, last) in enumerate(line_tiles(local_cols)):
        for k in range(first, last + 1):
            inside = (lane & 127) + (u * 128 - k * local_cols)
            wanted = jnp.where(lane >= 128, inside + 64, inside)
            picked = (source == wanted) & (inside >= 0) & (inside < local_cols)
            returns_ref[begin : begin + 128, :] = jnp.where(picked, 1.0, 0.0).astype(jnp.bfloat16)
            begin += 128

    for copy in copies:
        copy.wait()
    values = pair_ref[...].astype(jnp.float32)
    center = values - jnp.mean(values, axis=-1, keepdims=True)
    spread = jnp.mean(center * center, axis=-1, keepdims=True)
    normed = center * lax.rsqrt(spread + epsilon) * in_gain_ref[...] + in_bias_ref[...]
    normed = normed.astype(jnp.bfloat16)
    projected, gate = [
        lax.dot_general(weights[...], normed, (((0,), (1,)), ((), ())), preferred_element_type=jnp.float32)
        for weights in (w_proj_ref, w_gate_ref)
    ]
    left_gate, left, right_gate, right = [projected[n * hidden : (n + 1) * hidden] for n in range(4)]
    left = jax.nn.sigmoid(left_gate) * left
    right = jax.nn.sigmoid(right_gate) * right
    sides = [side[at : at + share] for at in range(0, hidden, share) for side in (left, right)]
    out_ref[...] = jnp.concatenate(sides, axis=0).astype(jnp.bfloat16)
    gating_ref[...] = jax.nn.sigmoid(gate)
    columns_ref[0] = jnp.broadcast_to(out_gain_ref[...], (128, hidden)).T
    columns_ref[1] = jnp.broadcast_to(out_bias_ref[...], (128, hidden)).T
    w_out_t_ref[...] = w_out_ref[...].astype(jnp.float32).T.astype(jnp.bfloat16)


def triangle_kernel(rows, inner, loops, local_rows, local_cols, pad, in_ref, out_ref, sides_ref, tri_ref):
    both = in_ref.shape[1]
    share = both // 2
    depth = inner * local_rows
    tiles = loops * pad // 128
    blank = jnp.zeros((both, pad - local_cols), jnp.float32)

    @pl.loop(0, inner)
    def unpack(r):
        blocks = [in_ref[l * inner + r].astype(jnp.float32) for l in range(loops)]
        for k in range(local_rows):
            line = []
            for block in blocks:
                line.append(block[:, k * local_cols : (k + 1) * local_cols])
                if pad > local_cols:
                    line.append(blank)
            line = jnp.concatenate(line, axis=1)
            for t in range(tiles):
                place = pl.ds(t * both * depth + r * local_rows + k, both, stride=depth)
                sides_ref[place, :] = line[:, t * 128 : (t + 1) * 128]

    def matrix(index):
        return jnp.concatenate(
            [sides_ref[pl.ds((t * both + index) * depth, depth), :] for t in range(tiles)], axis=1
        ).astype(jnp.bfloat16)

    for c in range(share):
        product = lax.dot_general(
            matrix(c), matrix(share + c), (((0,), (0,)), ((), ())), preferred_element_type=jnp.float32
        )
        for t in range(tiles):
            tri_ref[pl.ds((t * share + c) * loops * pad, loops * pad), :] = product[:, t * 128 : (t + 1) * 128]

    @pl.loop(0, rows)
    def pack(r):
        begin = r * local_rows
        begin = (begin // local_cols) * pad + begin % local_cols
        for l in range(loops):
            first, last = l * pad // 128, -(-(l * pad + local_cols) // 128)
            line = []
            for k in range(local_rows):
                here = [
                    tri_ref[pl.ds(t * share * loops * pad + begin + k, share, stride=loops * pad), :]
                    for t in range(first, last)
                ]
                offset = l * pad - first * 128
                line.append(jnp.concatenate(here, axis=1)[:, offset : offset + local_cols])
            out_ref[r * loops + l] = jnp.concatenate(line, axis=1).astype(jnp.bfloat16)


def line_triangle_kernel(inner, loops, local_rows, local_cols, in_ref, shifts_ref, returns_ref, out_ref, sides_ref, *tri_refs):
    both = in_ref.shape[1]
    share = both // 2
    depth = inner * local_rows
    pairs = loops // 2
    group = local_cols // local_rows
    height = depth + 8
    block = loops * local_rows + 8
    lane = lax.broadcasted_iota(jnp.int32, (inner * both, 128), 1)

    blocks = [jnp.concatenate([in_ref[l * inner + r] for r in range(inner)], axis=0) for l in range(loops)]
    period = math.lcm(local_cols, 128) // local_cols
    tiles = line_tiles(local_cols)
    for u, k, count in line_groups(local_cols):
        offset = k * local_cols % 128
        stack, target = [], []
        for pair in range(pairs):
            for turn in range(local_rows // period):
                line = []
                for side in blocks[2 * pair : 2 * pair + 2]:
                    at = (turn * len(tiles) + u) * 128
                    tile = side[:, at : at + 128]
                    if offset + local_cols > 128:
                        tile = jnp.where(lane >= offset, tile, side[:, at + 128 : at + 256])
                    line.append(tile)
                stack.append(jnp.concatenate(line, axis=1))
                target.append(pair * both * height + turn * period + k)
        lines = jnp.dot(
            jnp.concatenate(stack, axis=0),
            shifts_ref[:, k * 128 : (k + count) * 128],
            preferred_element_type=jnp.float32,
        )
        for m, place in enumerate(target):
            for r in range(inner):
                for part in range(0, both, 8):
                    first = (m * inner + r) * both + part
                    for n in range(count):
                        target_rows = pl.ds(place + part * height + r * local_rows + n, 8, stride=height)
                        sides_ref[target_rows, :] = lines[first : first + 8, n * 128 : (n + 1) * 128]

    def matrix(index):
        return jnp.concatenate(
            [sides_ref[pl.ds((t * both + index) * height, depth), :] for t in range(pairs)], axis=1
        ).astype(jnp.bfloat16)

    for t in range(pairs):
        for c in range(share):
            right = sides_ref[pl.ds((t * both + share + c) * height, depth), :].astype(jnp.bfloat16)
            product = lax.dot_general(
                matrix(c), right, (((0,), (0,)), ((), ())), preferred_element_type=jnp.float32
            )
            for h in range(group):
                for l in range(loops):
                    place = (h * share + c) * block + l * local_rows
                    first = l * 64 + h * local_rows
                    tri_refs[t][place : place + local_rows, :] = product[first : first + local_rows, :]

    members = group * share
    for t in range(pairs):

        def tri_line(l, k):
            parts = [
                tri_refs[t][pl.ds(part * block + l * local_rows + k, 8, stride=block), :]
                for part in range(0, members, 8)
            ]
            return jnp.concatenate(parts, axis=0).astype(jnp.bfloat16)

        begin = 0
        for u, (first, last) in enumerate(tiles):
            stack = [
                jnp.concatenate([tri_line(l, turn + k) for k in range(first, last + 1)], axis=1)
                for l in range(loops)
                for turn in range(0, local_rows, period)
            ]
            end = begin + (last + 1 - first) * 128
            lanes = jnp.dot(
                jnp.concatenate(stack, axis=0), returns_ref[begin:end, :], preferred_element_type=jnp.float32
            ).astype(jnp.bfloat16)
            begin = end
            for l in range(loops):
                for turn in range(local_rows // period):
                    place = (turn * len(tiles) + u) * 128
                    for h in range(group):
                        row = ((l * (local_rows // period) + turn) * group + h) * share
                        for side in range(2):
                            out_ref[(l * group + h) * loops + 2 * t + side, :, place : place + 128] = lanes[
                                row : row + share, side * 128 : (side + 1) * 128
                            ]


def make_sides(owners, local_cols, *given):
    places, channels = given[0].shape
    wide = given[1].shape[1]
    hidden = wide // 4
    returns = sum(last + 1 - first for first, last in line_tiles(local_cols))
    return pl.pallas_call(
        functools.partial(sides_kernel, owners, local_cols),
        out_shape=(
            jax.ShapeDtypeStruct((wide // 2, places), jnp.bfloat16),
            jax.ShapeDtypeStruct((channels, places), jnp.float32),
            jax.ShapeDtypeStruct((2, hidden, 128), jnp.float32),
            jax.ShapeDtypeStruct((channels, hidden), jnp.bfloat16),
            jax.ShapeDtypeStruct((256, math.lcm(local_cols, 128) // local_cols * 128), jnp.bfloat16),
            jax.ShapeDtypeStruct((returns * 128, 256), jnp.bfloat16),
        ),
        in_specs=[in_hbm] * len(given),
        out_specs=[in_vmem] * 6,
        scratch_shapes=[pltpu.VMEM(x.shape, x.dtype) for x in given] + [pltpu.SemaphoreType.DMA((len(given),))],
        compiler_params=pltpu.CompilerParams(vmem_limit_bytes=vmem_bytes),
        name="sides",
    )(*[pltpu.with_memory_space_constraint(x, pltpu.HBM) for x in given])


def update_kernel(inner, loops, tri_ref, gating_ref, columns_ref, w_ref, out_ref):
    values = tri_ref[0].astype(jnp.float32)
    for half in range(1, tri_ref.shape[0]):
        values += tri_ref[half].astype(jnp.float32)
    share = values.shape[0] // (inner * loops)
    starts = [(r * loops + l) * share for l in range(loops) for r in range(inner)]
    values = jnp.concatenate([values[start : start + share] for start in starts], axis=0)
    center = values - jnp.mean(values, axis=0, keepdims=True)
    spread = jnp.mean(center * center, axis=0, keepdims=True)
    mixed = center * lax.rsqrt(spread + epsilon) * columns_ref[0][:, :1] + columns_ref[1][:, :1]
    outgoing = jnp.dot(w_ref[...], mixed.astype(jnp.bfloat16), preferred_element_type=jnp.float32)
    out_ref[...] = (gating_ref[...] * outgoing).T.astype(jnp.bfloat16)


def make_update(inner, loops, triangle, gating, columns, w_out_t):
    channels, places = gating.shape
    return pl.pallas_call(
        functools.partial(update_kernel, inner, loops),
        out_shape=jax.ShapeDtypeStruct((places, channels), jnp.bfloat16),
        in_specs=[in_vmem] * 4,
        out_specs=in_vmem,
        compiler_params=pltpu.CompilerParams(vmem_limit_bytes=vmem_bytes),
        name="update",
    )(triangle, gating, columns, w_out_t)


def make_triangle(sides, shifts, returns, rows, inner, loops, local_rows, local_cols):
    owners, both, places = sides.shape
    share = both // 2
    operands = [sides]
    if in_lines(rows, loops, share, local_rows, local_cols):
        operands += [shifts, returns]
        kernel = functools.partial(line_triangle_kernel, inner, loops, local_rows, local_cols)
        sides_rows = (loops // 2 * both + 1) * (inner * local_rows + 8)
        tri_rows = [(share * (local_cols // local_rows) + 1) * (loops * local_rows + 8)] * (loops // 2)
    else:
        pad = 64 if local_cols <= 64 and loops % 2 == 0 else -(-local_cols // 128) * 128
        kernel = functools.partial(triangle_kernel, rows, inner, loops, local_rows, local_cols, pad)
        sides_rows = loops * pad // 128 * both * inner * local_rows
        tri_rows = [loops * pad // 128 * share * loops * pad]
    return pl.pallas_call(
        kernel,
        out_shape=jax.ShapeDtypeStruct((rows * loops, share, places), jnp.bfloat16),
        in_specs=[in_vmem] * len(operands),
        out_specs=in_vmem,
        scratch_shapes=[pltpu.VMEM((n, 128), jnp.float32) for n in [sides_rows] + tri_rows],
        compiler_params=pltpu.CompilerParams(vmem_limit_bytes=vmem_bytes),
        name="triangle",
    )(*operands)


def on_device(halves, inner, loops, pair, ln_in_gain, ln_in_bias, w_proj, w_gate, ln_out_gain, ln_out_bias, w_out):
    local_rows, local_cols, channels = pair.shape
    hidden = w_out.shape[0]
    owners = inner * loops
    share = hidden // owners
    places = local_rows * local_cols

    sides, gating, columns, w_out_t, shifts, returns = make_sides(
        owners,
        local_cols,
        pair.reshape(places, channels),
        w_proj,
        w_gate,
        ln_in_gain[None],
        ln_in_bias[None],
        ln_out_gain[None],
        ln_out_bias[None],
        w_out,
    )
    sides = lax.all_to_all(
        sides.reshape(owners, 2 * share, places), ("loop", "inner"), split_axis=0, concat_axis=0
    )
    triangle = make_triangle(
        sides, shifts, returns, halves * inner, inner, loops, local_rows, local_cols
    )
    triangle = lax.all_to_all(triangle, ("half", "inner", "loop"), split_axis=0, concat_axis=0)
    update = make_update(inner, loops, triangle.reshape(halves, hidden, places), gating, columns, w_out_t)
    return update.reshape(local_rows, local_cols, channels)


def solution(mesh):
    rows, loops = mesh.shape["row"], mesh.shape["loop"]
    halves = 2 if rows % 2 == 0 else 1
    inner = rows // halves
    split = Mesh(mesh.devices.reshape(halves, inner, loops), ("half", "inner", "loop"))
    placed = P(("half", "inner"), "loop", None)
    return jax.shard_map(
        lambda *arrays: on_device(halves, inner, loops, *arrays),
        mesh=split,
        in_specs=(placed, P(), P(), P(), P(), P(), P(), P()),
        out_specs=placed,
        check_vma=False,
    )
```

```python
import functools
import math

import jax
import jax.numpy as jnp
from jax import lax
from jax.experimental import pallas as pl
from jax.experimental.pallas import tpu as pltpu
from jax.sharding import Mesh
from jax.sharding import PartitionSpec as P

epsilon = 1e-05
in_vmem = pl.BlockSpec(memory_space=pltpu.VMEM)
in_hbm = pl.BlockSpec(memory_space=pltpu.HBM)
vmem_bytes = 48 * 2**20


def line_groups(local_cols):
    groups = []
    for k in range(math.lcm(local_cols, 128) // local_cols):
        tile, offset = divmod(k * local_cols, 128)
        over = offset + local_cols > 128
        if over or not groups or groups[-1][0] != tile:
            groups.append((tile, k, 1))
        else:
            groups[-1] = (tile, groups[-1][1], groups[-1][2] + 1)
    return groups


def line_tiles(local_cols):
    tiles = math.lcm(local_cols, 128) // 128
    return [(u * 128 // local_cols, ((u + 1) * 128 - 1) // local_cols) for u in range(tiles)]


def in_lines(rows, loops, share, local_rows, local_cols):
    return (
        local_cols <= 64
        and local_cols % local_rows == 0
        and local_rows % 8 == 0
        and local_rows % (math.lcm(local_cols, 128) // local_cols) == 0
        and loops % 2 == 0
        and rows * local_rows == loops * local_cols
        and share % 8 == 0
    )


def sides_kernel(owners, local_cols, *refs):
    given, results, held, sems = refs[:8], refs[8:14], refs[14:22], refs[22]
    out_ref, gating_ref, columns_ref, w_out_t_ref, shifts_ref, returns_ref = results
    copies = [pltpu.make_async_copy(*ends, sems.at[n]) for n, ends in enumerate(zip(given, held))]
    for copy in copies:
        copy.start()
    pair_ref, w_proj_ref, w_gate_ref, in_gain_ref, in_bias_ref, out_gain_ref, out_bias_ref, w_out_ref = held
    hidden = w_proj_ref.shape[1] // 4
    share = hidden // owners

    source = lax.broadcasted_iota(jnp.int32, (256, 128), 0)
    lane = lax.broadcasted_iota(jnp.int32, (256, 128), 1)
    for k in range(shifts_ref.shape[1] // 128):
        wanted = ((lane & 63) + k * local_cols % 128) & 127
        wanted = jnp.where(lane >= 64, wanted + 128, wanted)
        picked = (source == wanted) & ((lane & 63) < local_cols)
        shifts_ref[:, k * 128 : (k + 1) * 128] = jnp.where(picked, 1.0, 0.0).astype(jnp.bfloat16)

    source = lax.broadcasted_iota(jnp.int32, (128, 256), 0)
    lane = lax.broadcasted_iota(jnp.int32, (128, 256), 1)
    begin = 0
    for u, (first, last) in enumerate(line_tiles(local_cols)):
        for k in range(first, last + 1):
            inside = (lane & 127) + (u * 128 - k * local_cols)
            wanted = jnp.where(lane >= 128, inside + 64, inside)
            picked = (source == wanted) & (inside >= 0) & (inside < local_cols)
            returns_ref[begin : begin + 128, :] = jnp.where(picked, 1.0, 0.0).astype(jnp.bfloat16)
            begin += 128

    for copy in copies:
        copy.wait()
    values = pair_ref[...].astype(jnp.float32)
    center = values - jnp.mean(values, axis=-1, keepdims=True)
    spread = jnp.mean(center * center, axis=-1, keepdims=True)
    normed = center * lax.rsqrt(spread + epsilon) * in_gain_ref[...] + in_bias_ref[...]
    normed = normed.astype(jnp.bfloat16)
    projected, gate = [
        lax.dot_general(weights[...], normed, (((0,), (1,)), ((), ())), preferred_element_type=jnp.float32)
        for weights in (w_proj_ref, w_gate_ref)
    ]
    left_gate, left, right_gate, right = [projected[n * hidden : (n + 1) * hidden] for n in range(4)]
    left = jax.nn.sigmoid(left_gate) * left
    right = jax.nn.sigmoid(right_gate) * right
    sides = [side[at : at + share] for at in range(0, hidden, share) for side in (left, right)]
    out_ref[...] = jnp.concatenate(sides, axis=0).astype(jnp.bfloat16)
    gating_ref[...] = jax.nn.sigmoid(gate)
    columns_ref[0] = jnp.broadcast_to(out_gain_ref[...], (128, hidden)).T
    columns_ref[1] = jnp.broadcast_to(out_bias_ref[...], (128, hidden)).T
    w_out_t_ref[...] = w_out_ref[...].astype(jnp.float32).T.astype(jnp.bfloat16)


def triangle_kernel(rows, inner, loops, local_rows, local_cols, pad, in_ref, out_ref, sides_ref, tri_ref):
    both = in_ref.shape[1]
    share = both // 2
    depth = inner * local_rows
    tiles = loops * pad // 128
    blank = jnp.zeros((both, pad - local_cols), jnp.float32)

    @pl.loop(0, inner)
    def unpack(r):
        blocks = [in_ref[l * inner + r].astype(jnp.float32) for l in range(loops)]
        for k in range(local_rows):
            line = []
            for block in blocks:
                line.append(block[:, k * local_cols : (k + 1) * local_cols])
                if pad > local_cols:
                    line.append(blank)
            line = jnp.concatenate(line, axis=1)
            for t in range(tiles):
                place = pl.ds(t * both * depth + r * local_rows + k, both, stride=depth)
                sides_ref[place, :] = line[:, t * 128 : (t + 1) * 128]

    def matrix(index):
        return jnp.concatenate(
            [sides_ref[pl.ds((t * both + index) * depth, depth), :] for t in range(tiles)], axis=1
        ).astype(jnp.bfloat16)

    for c in range(share):
        product = lax.dot_general(
            matrix(c), matrix(share + c), (((0,), (0,)), ((), ())), preferred_element_type=jnp.float32
        )
        for t in range(tiles):
            tri_ref[pl.ds((t * share + c) * loops * pad, loops * pad), :] = product[:, t * 128 : (t + 1) * 128]

    @pl.loop(0, rows)
    def pack(r):
        begin = r * local_rows
        begin = (begin // local_cols) * pad + begin % local_cols
        for l in range(loops):
            first, last = l * pad // 128, -(-(l * pad + local_cols) // 128)
            line = []
            for k in range(local_rows):
                here = [
                    tri_ref[pl.ds(t * share * loops * pad + begin + k, share, stride=loops * pad), :]
                    for t in range(first, last)
                ]
                offset = l * pad - first * 128
                line.append(jnp.concatenate(here, axis=1)[:, offset : offset + local_cols])
            out_ref[r * loops + l] = jnp.concatenate(line, axis=1).astype(jnp.bfloat16)


def line_triangle_kernel(inner, loops, local_rows, local_cols, in_ref, shifts_ref, returns_ref, out_ref, sides_ref, *tri_refs):
    both = in_ref.shape[1]
    share = both // 2
    depth = inner * local_rows
    pairs = loops // 2
    group = local_cols // local_rows
    height = depth + 8
    block = loops * local_rows + 8
    lane = lax.broadcasted_iota(jnp.int32, (inner * both, 128), 1)

    blocks = [jnp.concatenate([in_ref[l * inner + r] for r in range(inner)], axis=0) for l in range(loops)]
    period = math.lcm(local_cols, 128) // local_cols
    tiles = line_tiles(local_cols)
    for u, k, count in line_groups(local_cols):
        offset = k * local_cols % 128
        stack, target = [], []
        for pair in range(pairs):
            for turn in range(local_rows // period):
                line = []
                for side in blocks[2 * pair : 2 * pair + 2]:
                    at = (turn * len(tiles) + u) * 128
                    tile = side[:, at : at + 128]
                    if offset + local_cols > 128:
                        tile = jnp.where(lane >= offset, tile, side[:, at + 128 : at + 256])
                    line.append(tile)
                stack.append(jnp.concatenate(line, axis=1))
                target.append(pair * both * height + turn * period + k)
        lines = jnp.dot(
            jnp.concatenate(stack, axis=0),
            shifts_ref[:, k * 128 : (k + count) * 128],
            preferred_element_type=jnp.float32,
        )
        for m, place in enumerate(target):
            for r in range(inner):
                for part in range(0, both, 8):
                    first = (m * inner + r) * both + part
                    for n in range(count):
                        target_rows = pl.ds(place + part * height + r * local_rows + n, 8, stride=height)
                        sides_ref[target_rows, :] = lines[first : first + 8, n * 128 : (n + 1) * 128]

    def matrix(index):
        return jnp.concatenate(
            [sides_ref[pl.ds((t * both + index) * height, depth), :] for t in range(pairs)], axis=1
        ).astype(jnp.bfloat16)

    for t in range(pairs):
        for c in range(share):
            right = sides_ref[pl.ds((t * both + share + c) * height, depth), :].astype(jnp.bfloat16)
            product = lax.dot_general(
                matrix(c), right, (((0,), (0,)), ((), ())), preferred_element_type=jnp.float32
            )
            for h in range(group):
                for l in range(loops):
                    place = (h * share + c) * block + l * local_rows
                    first = l * 64 + h * local_rows
                    tri_refs[t][place : place + local_rows, :] = product[first : first + local_rows, :]

    members = group * share
    for t in range(pairs):

        def tri_line(l, k):
            parts = [
                tri_refs[t][pl.ds(part * block + l * local_rows + k, 8, stride=block), :]
                for part in range(0, members, 8)
            ]
            return jnp.concatenate(parts, axis=0).astype(jnp.bfloat16)

        begin = 0
        for u, (first, last) in enumerate(tiles):
            stack = [
                jnp.concatenate([tri_line(l, turn + k) for k in range(first, last + 1)], axis=1)
                for l in range(loops)
                for turn in range(0, local_rows, period)
            ]
            end = begin + (last + 1 - first) * 128
            lanes = jnp.dot(
                jnp.concatenate(stack, axis=0), returns_ref[begin:end, :], preferred_element_type=jnp.float32
            ).astype(jnp.bfloat16)
            begin = end
            for l in range(loops):
                for turn in range(local_rows // period):
                    place = (turn * len(tiles) + u) * 128
                    for h in range(group):
                        row = ((l * (local_rows // period) + turn) * group + h) * share
                        for side in range(2):
                            out_ref[(l * group + h) * loops + 2 * t + side, :, place : place + 128] = lanes[
                                row : row + share, side * 128 : (side + 1) * 128
                            ]


def make_sides(owners, local_cols, *given):
    places, channels = given[0].shape
    wide = given[1].shape[1]
    hidden = wide // 4
    returns = sum(last + 1 - first for first, last in line_tiles(local_cols))
    return pl.pallas_call(
        functools.partial(sides_kernel, owners, local_cols),
        out_shape=(
            jax.ShapeDtypeStruct((wide // 2, places), jnp.bfloat16),
            jax.ShapeDtypeStruct((channels, places), jnp.float32),
            jax.ShapeDtypeStruct((2, hidden, 128), jnp.float32),
            jax.ShapeDtypeStruct((channels, hidden), jnp.bfloat16),
            jax.ShapeDtypeStruct((256, math.lcm(local_cols, 128) // local_cols * 128), jnp.bfloat16),
            jax.ShapeDtypeStruct((returns * 128, 256), jnp.bfloat16),
        ),
        in_specs=[in_hbm] * len(given),
        out_specs=[in_vmem] * 6,
        scratch_shapes=[pltpu.VMEM(x.shape, x.dtype) for x in given] + [pltpu.SemaphoreType.DMA((len(given),))],
        compiler_params=pltpu.CompilerParams(vmem_limit_bytes=vmem_bytes),
        name="sides",
    )(*[pltpu.with_memory_space_constraint(x, pltpu.HBM) for x in given])


def update_kernel(inner, loops, tri_ref, gating_ref, columns_ref, w_ref, out_ref):
    values = tri_ref[0].astype(jnp.float32)
    for half in range(1, tri_ref.shape[0]):
        values += tri_ref[half].astype(jnp.float32)
    share = values.shape[0] // (inner * loops)
    starts = [(r * loops + l) * share for l in range(loops) for r in range(inner)]
    values = jnp.concatenate([values[start : start + share] for start in starts], axis=0)
    center = values - jnp.mean(values, axis=0, keepdims=True)
    spread = jnp.mean(center * center, axis=0, keepdims=True)
    mixed = center * lax.rsqrt(spread + epsilon) * columns_ref[0][:, :1] + columns_ref[1][:, :1]
    outgoing = jnp.dot(w_ref[...], mixed.astype(jnp.bfloat16), preferred_element_type=jnp.float32)
    out_ref[...] = (gating_ref[...] * outgoing).astype(jnp.bfloat16).T


def make_update(inner, loops, triangle, gating, columns, w_out_t):
    channels, places = gating.shape
    return pl.pallas_call(
        functools.partial(update_kernel, inner, loops),
        out_shape=jax.ShapeDtypeStruct((places, channels), jnp.bfloat16),
        in_specs=[in_vmem] * 4,
        out_specs=in_vmem,
        compiler_params=pltpu.CompilerParams(vmem_limit_bytes=vmem_bytes),
        name="update",
    )(triangle, gating, columns, w_out_t)


def make_triangle(sides, shifts, returns, rows, inner, loops, local_rows, local_cols):
    owners, both, places = sides.shape
    share = both // 2
    operands = [sides]
    if in_lines(rows, loops, share, local_rows, local_cols):
        operands += [shifts, returns]
        kernel = functools.partial(line_triangle_kernel, inner, loops, local_rows, local_cols)
        sides_rows = (loops // 2 * both + 1) * (inner * local_rows + 8)
        tri_rows = [(share * (local_cols // local_rows) + 1) * (loops * local_rows + 8)] * (loops // 2)
    else:
        pad = 64 if local_cols <= 64 and loops % 2 == 0 else -(-local_cols // 128) * 128
        kernel = functools.partial(triangle_kernel, rows, inner, loops, local_rows, local_cols, pad)
        sides_rows = loops * pad // 128 * both * inner * local_rows
        tri_rows = [loops * pad // 128 * share * loops * pad]
    return pl.pallas_call(
        kernel,
        out_shape=jax.ShapeDtypeStruct((rows * loops, share, places), jnp.bfloat16),
        in_specs=[in_vmem] * len(operands),
        out_specs=in_vmem,
        scratch_shapes=[pltpu.VMEM((n, 128), jnp.float32) for n in [sides_rows] + tri_rows],
        compiler_params=pltpu.CompilerParams(vmem_limit_bytes=vmem_bytes),
        name="triangle",
    )(*operands)


def on_device(halves, inner, loops, pair, ln_in_gain, ln_in_bias, w_proj, w_gate, ln_out_gain, ln_out_bias, w_out):
    local_rows, local_cols, channels = pair.shape
    hidden = w_out.shape[0]
    owners = inner * loops
    share = hidden // owners
    places = local_rows * local_cols

    sides, gating, columns, w_out_t, shifts, returns = make_sides(
        owners,
        local_cols,
        pair.reshape(places, channels),
        w_proj,
        w_gate,
        ln_in_gain[None],
        ln_in_bias[None],
        ln_out_gain[None],
        ln_out_bias[None],
        w_out,
    )
    sides = lax.all_to_all(
        sides.reshape(owners, 2 * share, places), ("loop", "inner"), split_axis=0, concat_axis=0
    )
    triangle = make_triangle(
        sides, shifts, returns, halves * inner, inner, loops, local_rows, local_cols
    )
    triangle = lax.all_to_all(triangle, ("half", "inner", "loop"), split_axis=0, concat_axis=0)
    update = make_update(inner, loops, triangle.reshape(halves, hidden, places), gating, columns, w_out_t)
    return update.reshape(local_rows, local_cols, channels)


def solution(mesh):
    rows, loops = mesh.shape["row"], mesh.shape["loop"]
    halves = 2 if rows % 2 == 0 else 1
    inner = rows // halves
    split = Mesh(mesh.devices.reshape(halves, inner, loops), ("half", "inner", "loop"))
    placed = P(("half", "inner"), "loop", None)
    return jax.shard_map(
        lambda *arrays: on_device(halves, inner, loops, *arrays),
        mesh=split,
        in_specs=(placed, P(), P(), P(), P(), P(), P(), P()),
        out_specs=placed,
        check_vma=False,
    )
```

```python
import functools
import math

import jax
import jax.numpy as jnp
from jax import lax
from jax.experimental import pallas as pl
from jax.experimental.pallas import tpu as pltpu
from jax.sharding import Mesh
from jax.sharding import PartitionSpec as P

epsilon = 1e-05
in_vmem = pl.BlockSpec(memory_space=pltpu.VMEM)
in_hbm = pl.BlockSpec(memory_space=pltpu.HBM)
vmem_bytes = 48 * 2**20


def line_groups(local_cols):
    groups = []
    for k in range(math.lcm(local_cols, 128) // local_cols):
        tile, offset = divmod(k * local_cols, 128)
        over = offset + local_cols > 128
        if over or not groups or groups[-1][0] != tile:
            groups.append((tile, k, 1))
        else:
            groups[-1] = (tile, groups[-1][1], groups[-1][2] + 1)
    return groups


def line_tiles(local_cols):
    tiles = math.lcm(local_cols, 128) // 128
    return [(u * 128 // local_cols, ((u + 1) * 128 - 1) // local_cols) for u in range(tiles)]


def in_lines(rows, loops, share, local_rows, local_cols):
    return (
        local_cols <= 64
        and local_cols % local_rows == 0
        and local_rows % 8 == 0
        and local_rows % (math.lcm(local_cols, 128) // local_cols) == 0
        and loops % 2 == 0
        and rows * local_rows == loops * local_cols
        and share % 8 == 0
    )


def sides_kernel(owners, local_cols, *refs):
    given, results, held, sems = refs[:8], refs[8:14], refs[14:22], refs[22]
    out_ref, gating_ref, columns_ref, w_out_t_ref, shifts_ref, returns_ref = results
    copies = [pltpu.make_async_copy(*ends, sems.at[n]) for n, ends in enumerate(zip(given, held))]
    for copy in copies:
        copy.start()
    pair_ref, w_proj_ref, w_gate_ref, in_gain_ref, in_bias_ref, out_gain_ref, out_bias_ref, w_out_ref = held
    hidden = w_proj_ref.shape[1] // 4
    share = hidden // owners

    source = lax.broadcasted_iota(jnp.int32, (256, 128), 0)
    lane = lax.broadcasted_iota(jnp.int32, (256, 128), 1)
    for k in range(shifts_ref.shape[1] // 128):
        wanted = ((lane & 63) + k * local_cols % 128) & 127
        wanted = jnp.where(lane >= 64, wanted + 128, wanted)
        picked = (source == wanted) & ((lane & 63) < local_cols)
        shifts_ref[:, k * 128 : (k + 1) * 128] = jnp.where(picked, 1.0, 0.0).astype(jnp.bfloat16)

    source = lax.broadcasted_iota(jnp.int32, (128, 256), 0)
    lane = lax.broadcasted_iota(jnp.int32, (128, 256), 1)
    begin = 0
    for u, (first, last) in enumerate(line_tiles(local_cols)):
        for k in range(first, last + 1):
            inside = (lane & 127) + (u * 128 - k * local_cols)
            wanted = jnp.where(lane >= 128, inside + 64, inside)
            picked = (source == wanted) & (inside >= 0) & (inside < local_cols)
            returns_ref[begin : begin + 128, :] = jnp.where(picked, 1.0, 0.0).astype(jnp.bfloat16)
            begin += 128

    for copy in copies:
        copy.wait()
    values = pair_ref[...].astype(jnp.float32)
    center = values - jnp.mean(values, axis=-1, keepdims=True)
    spread = jnp.mean(center * center, axis=-1, keepdims=True)
    normed = center * lax.rsqrt(spread + epsilon) * in_gain_ref[...] + in_bias_ref[...]
    normed = normed.astype(jnp.bfloat16)
    weights = jnp.concatenate([w_proj_ref[...], w_gate_ref[...]], axis=1)
    projected = lax.dot_general(weights, normed, (((0,), (1,)), ((), ())), preferred_element_type=jnp.float32)
    left_gate, left, right_gate, right = [projected[n * hidden : (n + 1) * hidden] for n in range(4)]
    gate = projected[4 * hidden :]
    left = jax.nn.sigmoid(left_gate) * left
    right = jax.nn.sigmoid(right_gate) * right
    sides = [side[at : at + share] for at in range(0, hidden, share) for side in (left, right)]
    out_ref[...] = jnp.concatenate(sides, axis=0).astype(jnp.bfloat16)
    gating_ref[...] = jax.nn.sigmoid(gate)
    columns_ref[0] = jnp.broadcast_to(out_gain_ref[...], (128, hidden)).T
    columns_ref[1] = jnp.broadcast_to(out_bias_ref[...], (128, hidden)).T
    w_out_t_ref[...] = w_out_ref[...].astype(jnp.float32).T.astype(jnp.bfloat16)


def triangle_kernel(rows, inner, loops, local_rows, local_cols, pad, in_ref, out_ref, sides_ref, tri_ref):
    both = in_ref.shape[1]
    share = both // 2
    depth = inner * local_rows
    tiles = loops * pad // 128
    blank = jnp.zeros((both, pad - local_cols), jnp.float32)

    @pl.loop(0, inner)
    def unpack(r):
        blocks = [in_ref[l * inner + r].astype(jnp.float32) for l in range(loops)]
        for k in range(local_rows):
            line = []
            for block in blocks:
                line.append(block[:, k * local_cols : (k + 1) * local_cols])
                if pad > local_cols:
                    line.append(blank)
            line = jnp.concatenate(line, axis=1)
            for t in range(tiles):
                place = pl.ds(t * both * depth + r * local_rows + k, both, stride=depth)
                sides_ref[place, :] = line[:, t * 128 : (t + 1) * 128]

    def matrix(index):
        return jnp.concatenate(
            [sides_ref[pl.ds((t * both + index) * depth, depth), :] for t in range(tiles)], axis=1
        ).astype(jnp.bfloat16)

    for c in range(share):
        product = lax.dot_general(
            matrix(c), matrix(share + c), (((0,), (0,)), ((), ())), preferred_element_type=jnp.float32
        )
        for t in range(tiles):
            tri_ref[pl.ds((t * share + c) * loops * pad, loops * pad), :] = product[:, t * 128 : (t + 1) * 128]

    @pl.loop(0, rows)
    def pack(r):
        begin = r * local_rows
        begin = (begin // local_cols) * pad + begin % local_cols
        for l in range(loops):
            first, last = l * pad // 128, -(-(l * pad + local_cols) // 128)
            line = []
            for k in range(local_rows):
                here = [
                    tri_ref[pl.ds(t * share * loops * pad + begin + k, share, stride=loops * pad), :]
                    for t in range(first, last)
                ]
                offset = l * pad - first * 128
                line.append(jnp.concatenate(here, axis=1)[:, offset : offset + local_cols])
            out_ref[r * loops + l] = jnp.concatenate(line, axis=1).astype(jnp.bfloat16)


def line_triangle_kernel(inner, loops, local_rows, local_cols, in_ref, shifts_ref, returns_ref, out_ref, sides_ref, *tri_refs):
    both = in_ref.shape[1]
    share = both // 2
    depth = inner * local_rows
    pairs = loops // 2
    group = local_cols // local_rows
    height = depth + 8
    block = loops * local_rows + 8
    lane = lax.broadcasted_iota(jnp.int32, (inner * both, 128), 1)

    blocks = [jnp.concatenate([in_ref[l * inner + r] for r in range(inner)], axis=0) for l in range(loops)]
    period = math.lcm(local_cols, 128) // local_cols
    tiles = line_tiles(local_cols)
    for u, k, count in line_groups(local_cols):
        offset = k * local_cols % 128
        stack, target = [], []
        for pair in range(pairs):
            for turn in range(local_rows // period):
                line = []
                for side in blocks[2 * pair : 2 * pair + 2]:
                    at = (turn * len(tiles) + u) * 128
                    tile = side[:, at : at + 128]
                    if offset + local_cols > 128:
                        tile = jnp.where(lane >= offset, tile, side[:, at + 128 : at + 256])
                    line.append(tile)
                stack.append(jnp.concatenate(line, axis=1))
                target.append(pair * both * height + turn * period + k)
        lines = jnp.dot(
            jnp.concatenate(stack, axis=0),
            shifts_ref[:, k * 128 : (k + count) * 128],
            preferred_element_type=jnp.float32,
        )
        for m, place in enumerate(target):
            for r in range(inner):
                for part in range(0, both, 8):
                    first = (m * inner + r) * both + part
                    for n in range(count):
                        target_rows = pl.ds(place + part * height + r * local_rows + n, 8, stride=height)
                        sides_ref[target_rows, :] = lines[first : first + 8, n * 128 : (n + 1) * 128]

    def matrix(index):
        return jnp.concatenate(
            [sides_ref[pl.ds((t * both + index) * height, depth), :] for t in range(pairs)], axis=1
        ).astype(jnp.bfloat16)

    for t in range(pairs):
        for c in range(share):
            right = sides_ref[pl.ds((t * both + share + c) * height, depth), :].astype(jnp.bfloat16)
            product = lax.dot_general(
                matrix(c), right, (((0,), (0,)), ((), ())), preferred_element_type=jnp.float32
            )
            for h in range(group):
                for l in range(loops):
                    place = (h * share + c) * block + l * local_rows
                    first = l * 64 + h * local_rows
                    tri_refs[t][place : place + local_rows, :] = product[first : first + local_rows, :]

    members = group * share
    for t in range(pairs):

        def tri_line(l, k):
            parts = [
                tri_refs[t][pl.ds(part * block + l * local_rows + k, 8, stride=block), :]
                for part in range(0, members, 8)
            ]
            return jnp.concatenate(parts, axis=0).astype(jnp.bfloat16)

        begin = 0
        for u, (first, last) in enumerate(tiles):
            stack = [
                jnp.concatenate([tri_line(l, turn + k) for k in range(first, last + 1)], axis=1)
                for l in range(loops)
                for turn in range(0, local_rows, period)
            ]
            end = begin + (last + 1 - first) * 128
            lanes = jnp.dot(
                jnp.concatenate(stack, axis=0), returns_ref[begin:end, :], preferred_element_type=jnp.float32
            ).astype(jnp.bfloat16)
            begin = end
            for l in range(loops):
                for turn in range(local_rows // period):
                    place = (turn * len(tiles) + u) * 128
                    for h in range(group):
                        row = ((l * (local_rows // period) + turn) * group + h) * share
                        for side in range(2):
                            out_ref[(l * group + h) * loops + 2 * t + side, :, place : place + 128] = lanes[
                                row : row + share, side * 128 : (side + 1) * 128
                            ]


def make_sides(owners, local_cols, *given):
    places, channels = given[0].shape
    wide = given[1].shape[1]
    hidden = wide // 4
    returns = sum(last + 1 - first for first, last in line_tiles(local_cols))
    return pl.pallas_call(
        functools.partial(sides_kernel, owners, local_cols),
        out_shape=(
            jax.ShapeDtypeStruct((wide // 2, places), jnp.bfloat16),
            jax.ShapeDtypeStruct((channels, places), jnp.float32),
            jax.ShapeDtypeStruct((2, hidden, 128), jnp.float32),
            jax.ShapeDtypeStruct((channels, hidden), jnp.bfloat16),
            jax.ShapeDtypeStruct((256, math.lcm(local_cols, 128) // local_cols * 128), jnp.bfloat16),
            jax.ShapeDtypeStruct((returns * 128, 256), jnp.bfloat16),
        ),
        in_specs=[in_hbm] * len(given),
        out_specs=[in_vmem] * 6,
        scratch_shapes=[pltpu.VMEM(x.shape, x.dtype) for x in given] + [pltpu.SemaphoreType.DMA((len(given),))],
        compiler_params=pltpu.CompilerParams(vmem_limit_bytes=vmem_bytes),
        name="sides",
    )(*[pltpu.with_memory_space_constraint(x, pltpu.HBM) for x in given])


def update_kernel(inner, loops, tri_ref, gating_ref, columns_ref, w_ref, out_ref):
    values = tri_ref[0].astype(jnp.float32)
    for half in range(1, tri_ref.shape[0]):
        values += tri_ref[half].astype(jnp.float32)
    share = values.shape[0] // (inner * loops)
    starts = [(r * loops + l) * share for l in range(loops) for r in range(inner)]
    values = jnp.concatenate([values[start : start + share] for start in starts], axis=0)
    center = values - jnp.mean(values, axis=0, keepdims=True)
    spread = jnp.mean(center * center, axis=0, keepdims=True)
    mixed = center * lax.rsqrt(spread + epsilon) * columns_ref[0][:, :1] + columns_ref[1][:, :1]
    outgoing = jnp.dot(w_ref[...], mixed.astype(jnp.bfloat16), preferred_element_type=jnp.float32)
    out_ref[...] = (gating_ref[...] * outgoing).astype(jnp.bfloat16).T


def make_update(inner, loops, triangle, gating, columns, w_out_t):
    channels, places = gating.shape
    return pl.pallas_call(
        functools.partial(update_kernel, inner, loops),
        out_shape=jax.ShapeDtypeStruct((places, channels), jnp.bfloat16),
        in_specs=[in_vmem] * 4,
        out_specs=in_vmem,
        compiler_params=pltpu.CompilerParams(vmem_limit_bytes=vmem_bytes),
        name="update",
    )(triangle, gating, columns, w_out_t)


def make_triangle(sides, shifts, returns, rows, inner, loops, local_rows, local_cols):
    owners, both, places = sides.shape
    share = both // 2
    operands = [sides]
    if in_lines(rows, loops, share, local_rows, local_cols):
        operands += [shifts, returns]
        kernel = functools.partial(line_triangle_kernel, inner, loops, local_rows, local_cols)
        sides_rows = (loops // 2 * both + 1) * (inner * local_rows + 8)
        tri_rows = [(share * (local_cols // local_rows) + 1) * (loops * local_rows + 8)] * (loops // 2)
    else:
        pad = 64 if local_cols <= 64 and loops % 2 == 0 else -(-local_cols // 128) * 128
        kernel = functools.partial(triangle_kernel, rows, inner, loops, local_rows, local_cols, pad)
        sides_rows = loops * pad // 128 * both * inner * local_rows
        tri_rows = [loops * pad // 128 * share * loops * pad]
    return pl.pallas_call(
        kernel,
        out_shape=jax.ShapeDtypeStruct((rows * loops, share, places), jnp.bfloat16),
        in_specs=[in_vmem] * len(operands),
        out_specs=in_vmem,
        scratch_shapes=[pltpu.VMEM((n, 128), jnp.float32) for n in [sides_rows] + tri_rows],
        compiler_params=pltpu.CompilerParams(vmem_limit_bytes=vmem_bytes),
        name="triangle",
    )(*operands)


def on_device(halves, inner, loops, pair, ln_in_gain, ln_in_bias, w_proj, w_gate, ln_out_gain, ln_out_bias, w_out):
    local_rows, local_cols, channels = pair.shape
    hidden = w_out.shape[0]
    owners = inner * loops
    share = hidden // owners
    places = local_rows * local_cols

    sides, gating, columns, w_out_t, shifts, returns = make_sides(
        owners,
        local_cols,
        pair.reshape(places, channels),
        w_proj,
        w_gate,
        ln_in_gain[None],
        ln_in_bias[None],
        ln_out_gain[None],
        ln_out_bias[None],
        w_out,
    )
    sides = lax.all_to_all(
        sides.reshape(owners, 2 * share, places), ("loop", "inner"), split_axis=0, concat_axis=0
    )
    triangle = make_triangle(
        sides, shifts, returns, halves * inner, inner, loops, local_rows, local_cols
    )
    triangle = lax.all_to_all(triangle, ("half", "inner", "loop"), split_axis=0, concat_axis=0)
    update = make_update(inner, loops, triangle.reshape(halves, hidden, places), gating, columns, w_out_t)
    return update.reshape(local_rows, local_cols, channels)


def solution(mesh):
    rows, loops = mesh.shape["row"], mesh.shape["loop"]
    halves = 2 if rows % 2 == 0 else 1
    inner = rows // halves
    split = Mesh(mesh.devices.reshape(halves, inner, loops), ("half", "inner", "loop"))
    placed = P(("half", "inner"), "loop", None)
    return jax.shard_map(
        lambda *arrays: on_device(halves, inner, loops, *arrays),
        mesh=split,
        in_specs=(placed, P(), P(), P(), P(), P(), P(), P()),
        out_specs=placed,
        check_vma=False,
    )
```

```python
import functools
import math

import jax
import jax.numpy as jnp
from jax import lax
from jax.experimental import pallas as pl
from jax.experimental.pallas import tpu as pltpu
from jax.sharding import Mesh
from jax.sharding import PartitionSpec as P

epsilon = 1e-05
in_vmem = pl.BlockSpec(memory_space=pltpu.VMEM)
in_hbm = pl.BlockSpec(memory_space=pltpu.HBM)
vmem_bytes = 48 * 2**20


def line_groups(local_cols):
    groups = []
    for k in range(math.lcm(local_cols, 128) // local_cols):
        tile, offset = divmod(k * local_cols, 128)
        over = offset + local_cols > 128
        if over or not groups or groups[-1][0] != tile:
            groups.append((tile, k, 1))
        else:
            groups[-1] = (tile, groups[-1][1], groups[-1][2] + 1)
    return groups


def line_tiles(local_cols):
    tiles = math.lcm(local_cols, 128) // 128
    return [(u * 128 // local_cols, ((u + 1) * 128 - 1) // local_cols) for u in range(tiles)]


def in_lines(rows, loops, share, local_rows, local_cols):
    return (
        local_cols <= 64
        and local_cols % local_rows == 0
        and local_rows % 8 == 0
        and local_rows % (math.lcm(local_cols, 128) // local_cols) == 0
        and loops % 2 == 0
        and rows * local_rows == loops * local_cols
        and share % 8 == 0
    )


def sides_kernel(owners, local_cols, *refs):
    given, results, held, sems = refs[:8], refs[8:14], refs[14:22], refs[22]
    out_ref, gating_ref, columns_ref, w_out_t_ref, shifts_ref, returns_ref = results
    copies = [pltpu.make_async_copy(*ends, sems.at[n]) for n, ends in enumerate(zip(given, held))]
    for copy in copies:
        copy.start()
    pair_ref, w_proj_ref, w_gate_ref, in_gain_ref, in_bias_ref, out_gain_ref, out_bias_ref, w_out_ref = held
    hidden = w_proj_ref.shape[1] // 4
    share = hidden // owners

    source = lax.broadcasted_iota(jnp.int32, (256, 128), 0)
    lane = lax.broadcasted_iota(jnp.int32, (256, 128), 1)
    for k in range(shifts_ref.shape[1] // 128):
        wanted = ((lane & 63) + k * local_cols % 128) & 127
        wanted = jnp.where(lane >= 64, wanted + 128, wanted)
        picked = (source == wanted) & ((lane & 63) < local_cols)
        shifts_ref[:, k * 128 : (k + 1) * 128] = jnp.where(picked, 1.0, 0.0).astype(jnp.bfloat16)

    source = lax.broadcasted_iota(jnp.int32, (128, 256), 0)
    lane = lax.broadcasted_iota(jnp.int32, (128, 256), 1)
    begin = 0
    for u, (first, last) in enumerate(line_tiles(local_cols)):
        for k in range(first, last + 1):
            inside = (lane & 127) + (u * 128 - k * local_cols)
            wanted = jnp.where(lane >= 128, inside + 64, inside)
            picked = (source == wanted) & (inside >= 0) & (inside < local_cols)
            returns_ref[begin : begin + 128, :] = jnp.where(picked, 1.0, 0.0).astype(jnp.bfloat16)
            begin += 128

    for copy in copies[5:]:
        copy.wait()
    columns_ref[0] = jnp.broadcast_to(out_gain_ref[...], (128, hidden)).T
    columns_ref[1] = jnp.broadcast_to(out_bias_ref[...], (128, hidden)).T
    w_out_t_ref[...] = w_out_ref[...].astype(jnp.float32).T.astype(jnp.bfloat16)
    for copy in copies[:5]:
        copy.wait()
    values = pair_ref[...].astype(jnp.float32)
    center = values - jnp.mean(values, axis=-1, keepdims=True)
    spread = jnp.mean(center * center, axis=-1, keepdims=True)
    normed = center * lax.rsqrt(spread + epsilon) * in_gain_ref[...] + in_bias_ref[...]
    normed = normed.astype(jnp.bfloat16)
    projected, gate = [
        lax.dot_general(weights[...], normed, (((0,), (1,)), ((), ())), preferred_element_type=jnp.float32)
        for weights in (w_proj_ref, w_gate_ref)
    ]
    left_gate, left, right_gate, right = [projected[n * hidden : (n + 1) * hidden] for n in range(4)]
    left = jax.nn.sigmoid(left_gate) * left
    right = jax.nn.sigmoid(right_gate) * right
    sides = [side[at : at + share] for at in range(0, hidden, share) for side in (left, right)]
    out_ref[...] = jnp.concatenate(sides, axis=0).astype(jnp.bfloat16)
    gating_ref[...] = jax.nn.sigmoid(gate)


def triangle_kernel(rows, inner, loops, local_rows, local_cols, pad, in_ref, out_ref, sides_ref, tri_ref):
    both = in_ref.shape[1]
    share = both // 2
    depth = inner * local_rows
    tiles = loops * pad // 128
    blank = jnp.zeros((both, pad - local_cols), jnp.float32)

    @pl.loop(0, inner)
    def unpack(r):
        blocks = [in_ref[l * inner + r].astype(jnp.float32) for l in range(loops)]
        for k in range(local_rows):
            line = []
            for block in blocks:
                line.append(block[:, k * local_cols : (k + 1) * local_cols])
                if pad > local_cols:
                    line.append(blank)
            line = jnp.concatenate(line, axis=1)
            for t in range(tiles):
                place = pl.ds(t * both * depth + r * local_rows + k, both, stride=depth)
                sides_ref[place, :] = line[:, t * 128 : (t + 1) * 128]

    def matrix(index):
        return jnp.concatenate(
            [sides_ref[pl.ds((t * both + index) * depth, depth), :] for t in range(tiles)], axis=1
        ).astype(jnp.bfloat16)

    for c in range(share):
        product = lax.dot_general(
            matrix(c), matrix(share + c), (((0,), (0,)), ((), ())), preferred_element_type=jnp.float32
        )
        for t in range(tiles):
            tri_ref[pl.ds((t * share + c) * loops * pad, loops * pad), :] = product[:, t * 128 : (t + 1) * 128]

    @pl.loop(0, rows)
    def pack(r):
        begin = r * local_rows
        begin = (begin // local_cols) * pad + begin % local_cols
        for l in range(loops):
            first, last = l * pad // 128, -(-(l * pad + local_cols) // 128)
            line = []
            for k in range(local_rows):
                here = [
                    tri_ref[pl.ds(t * share * loops * pad + begin + k, share, stride=loops * pad), :]
                    for t in range(first, last)
                ]
                offset = l * pad - first * 128
                line.append(jnp.concatenate(here, axis=1)[:, offset : offset + local_cols])
            out_ref[r * loops + l] = jnp.concatenate(line, axis=1).astype(jnp.bfloat16)


def line_triangle_kernel(inner, loops, local_rows, local_cols, in_ref, shifts_ref, returns_ref, out_ref, sides_ref, *tri_refs):
    both = in_ref.shape[1]
    share = both // 2
    depth = inner * local_rows
    pairs = loops // 2
    group = local_cols // local_rows
    height = depth + 8
    block = loops * local_rows + 8
    lane = lax.broadcasted_iota(jnp.int32, (inner * both, 128), 1)

    blocks = [jnp.concatenate([in_ref[l * inner + r] for r in range(inner)], axis=0) for l in range(loops)]
    period = math.lcm(local_cols, 128) // local_cols
    tiles = line_tiles(local_cols)
    for u, k, count in line_groups(local_cols):
        offset = k * local_cols % 128
        stack, target = [], []
        for pair in range(pairs):
            for turn in range(local_rows // period):
                line = []
                for side in blocks[2 * pair : 2 * pair + 2]:
                    at = (turn * len(tiles) + u) * 128
                    tile = side[:, at : at + 128]
                    if offset + local_cols > 128:
                        tile = jnp.where(lane >= offset, tile, side[:, at + 128 : at + 256])
                    line.append(tile)
                stack.append(jnp.concatenate(line, axis=1))
                target.append(pair * both * height + turn * period + k)
        lines = jnp.dot(
            jnp.concatenate(stack, axis=0),
            shifts_ref[:, k * 128 : (k + count) * 128],
            preferred_element_type=jnp.float32,
        )
        for m, place in enumerate(target):
            for r in range(inner):
                for part in range(0, both, 8):
                    first = (m * inner + r) * both + part
                    for n in range(count):
                        target_rows = pl.ds(place + part * height + r * local_rows + n, 8, stride=height)
                        sides_ref[target_rows, :] = lines[first : first + 8, n * 128 : (n + 1) * 128]

    def matrix(index):
        return jnp.concatenate(
            [sides_ref[pl.ds((t * both + index) * height, depth), :] for t in range(pairs)], axis=1
        ).astype(jnp.bfloat16)

    for t in range(pairs):
        for c in range(share):
            right = sides_ref[pl.ds((t * both + share + c) * height, depth), :].astype(jnp.bfloat16)
            product = lax.dot_general(
                matrix(c), right, (((0,), (0,)), ((), ())), preferred_element_type=jnp.float32
            )
            for h in range(group):
                for l in range(loops):
                    place = (h * share + c) * block + l * local_rows
                    first = l * 64 + h * local_rows
                    tri_refs[t][place : place + local_rows, :] = product[first : first + local_rows, :]

    members = group * share
    for t in range(pairs):

        def tri_line(l, k):
            parts = [
                tri_refs[t][pl.ds(part * block + l * local_rows + k, 8, stride=block), :]
                for part in range(0, members, 8)
            ]
            return jnp.concatenate(parts, axis=0).astype(jnp.bfloat16)

        begin = 0
        for u, (first, last) in enumerate(tiles):
            stack = [
                jnp.concatenate([tri_line(l, turn + k) for k in range(first, last + 1)], axis=1)
                for l in range(loops)
                for turn in range(0, local_rows, period)
            ]
            end = begin + (last + 1 - first) * 128
            lanes = jnp.dot(
                jnp.concatenate(stack, axis=0), returns_ref[begin:end, :], preferred_element_type=jnp.float32
            ).astype(jnp.bfloat16)
            begin = end
            for l in range(loops):
                for turn in range(local_rows // period):
                    place = (turn * len(tiles) + u) * 128
                    for h in range(group):
                        row = ((l * (local_rows // period) + turn) * group + h) * share
                        for side in range(2):
                            out_ref[(l * group + h) * loops + 2 * t + side, :, place : place + 128] = lanes[
                                row : row + share, side * 128 : (side + 1) * 128
                            ]


def make_sides(owners, local_cols, *given):
    places, channels = given[0].shape
    wide = given[1].shape[1]
    hidden = wide // 4
    returns = sum(last + 1 - first for first, last in line_tiles(local_cols))
    return pl.pallas_call(
        functools.partial(sides_kernel, owners, local_cols),
        out_shape=(
            jax.ShapeDtypeStruct((wide // 2, places), jnp.bfloat16),
            jax.ShapeDtypeStruct((channels, places), jnp.float32),
            jax.ShapeDtypeStruct((2, hidden, 128), jnp.float32),
            jax.ShapeDtypeStruct((channels, hidden), jnp.bfloat16),
            jax.ShapeDtypeStruct((256, math.lcm(local_cols, 128) // local_cols * 128), jnp.bfloat16),
            jax.ShapeDtypeStruct((returns * 128, 256), jnp.bfloat16),
        ),
        in_specs=[in_hbm] * len(given),
        out_specs=[in_vmem] * 6,
        scratch_shapes=[pltpu.VMEM(x.shape, x.dtype) for x in given] + [pltpu.SemaphoreType.DMA((len(given),))],
        compiler_params=pltpu.CompilerParams(vmem_limit_bytes=vmem_bytes),
        name="sides",
    )(*[pltpu.with_memory_space_constraint(x, pltpu.HBM) for x in given])


def update_kernel(inner, loops, tri_ref, gating_ref, columns_ref, w_ref, out_ref):
    values = tri_ref[0].astype(jnp.float32)
    for half in range(1, tri_ref.shape[0]):
        values += tri_ref[half].astype(jnp.float32)
    share = values.shape[0] // (inner * loops)
    starts = [(r * loops + l) * share for l in range(loops) for r in range(inner)]
    values = jnp.concatenate([values[start : start + share] for start in starts], axis=0)
    center = values - jnp.mean(values, axis=0, keepdims=True)
    spread = jnp.mean(center * center, axis=0, keepdims=True)
    mixed = center * lax.rsqrt(spread + epsilon) * columns_ref[0][:, :1] + columns_ref[1][:, :1]
    outgoing = jnp.dot(w_ref[...], mixed.astype(jnp.bfloat16), preferred_element_type=jnp.float32)
    out_ref[...] = (gating_ref[...] * outgoing).astype(jnp.bfloat16).T


def make_update(inner, loops, triangle, gating, columns, w_out_t):
    channels, places = gating.shape
    return pl.pallas_call(
        functools.partial(update_kernel, inner, loops),
        out_shape=jax.ShapeDtypeStruct((places, channels), jnp.bfloat16),
        in_specs=[in_vmem] * 4,
        out_specs=in_vmem,
        compiler_params=pltpu.CompilerParams(vmem_limit_bytes=vmem_bytes),
        name="update",
    )(triangle, gating, columns, w_out_t)


def make_triangle(sides, shifts, returns, rows, inner, loops, local_rows, local_cols):
    owners, both, places = sides.shape
    share = both // 2
    operands = [sides]
    if in_lines(rows, loops, share, local_rows, local_cols):
        operands += [shifts, returns]
        kernel = functools.partial(line_triangle_kernel, inner, loops, local_rows, local_cols)
        sides_rows = (loops // 2 * both + 1) * (inner * local_rows + 8)
        tri_rows = [(share * (local_cols // local_rows) + 1) * (loops * local_rows + 8)] * (loops // 2)
    else:
        pad = 64 if local_cols <= 64 and loops % 2 == 0 else -(-local_cols // 128) * 128
        kernel = functools.partial(triangle_kernel, rows, inner, loops, local_rows, local_cols, pad)
        sides_rows = loops * pad // 128 * both * inner * local_rows
        tri_rows = [loops * pad // 128 * share * loops * pad]
    return pl.pallas_call(
        kernel,
        out_shape=jax.ShapeDtypeStruct((rows * loops, share, places), jnp.bfloat16),
        in_specs=[in_vmem] * len(operands),
        out_specs=in_vmem,
        scratch_shapes=[pltpu.VMEM((n, 128), jnp.float32) for n in [sides_rows] + tri_rows],
        compiler_params=pltpu.CompilerParams(vmem_limit_bytes=vmem_bytes),
        name="triangle",
    )(*operands)


def on_device(halves, inner, loops, pair, ln_in_gain, ln_in_bias, w_proj, w_gate, ln_out_gain, ln_out_bias, w_out):
    local_rows, local_cols, channels = pair.shape
    hidden = w_out.shape[0]
    owners = inner * loops
    share = hidden // owners
    places = local_rows * local_cols

    sides, gating, columns, w_out_t, shifts, returns = make_sides(
        owners,
        local_cols,
        pair.reshape(places, channels),
        w_proj,
        w_gate,
        ln_in_gain[None],
        ln_in_bias[None],
        ln_out_gain[None],
        ln_out_bias[None],
        w_out,
    )
    sides = lax.all_to_all(
        sides.reshape(owners, 2 * share, places), ("loop", "inner"), split_axis=0, concat_axis=0
    )
    triangle = make_triangle(
        sides, shifts, returns, halves * inner, inner, loops, local_rows, local_cols
    )
    triangle = lax.all_to_all(triangle, ("half", "inner", "loop"), split_axis=0, concat_axis=0)
    update = make_update(inner, loops, triangle.reshape(halves, hidden, places), gating, columns, w_out_t)
    return update.reshape(local_rows, local_cols, channels)


def solution(mesh):
    rows, loops = mesh.shape["row"], mesh.shape["loop"]
    halves = 2 if rows % 2 == 0 else 1
    inner = rows // halves
    split = Mesh(mesh.devices.reshape(halves, inner, loops), ("half", "inner", "loop"))
    placed = P(("half", "inner"), "loop", None)
    return jax.shard_map(
        lambda *arrays: on_device(halves, inner, loops, *arrays),
        mesh=split,
        in_specs=(placed, P(), P(), P(), P(), P(), P(), P()),
        out_specs=placed,
        check_vma=False,
    )
```
